32 devices in a mesh: prow: 4 (over y, core), pcol: 8 (over z, x).
Axes of the slice: x: 2, y: 2, z: 4, core: 2. Of those that a mesh axis runs over, the one named last changes fastest.
Arguments:
- matrix: bfloat16 [4096, 4096], P('prow', 'pcol'), may hold values from -6 to 6
- panels: bfloat16 [4, 256, 4096], P(None, 'pcol', 'prow'), may hold values from -0.375 to 0.375
- exponents: int32 [4, 32], P(None, 'prow'), may hold values from -3 to 1
- inverses: bfloat16 [4, 256, 256], replicated, as said below
- pivots: int32 [4, 256], replicated, may hold values from 1024 to 4095, as said below
Outputs:
- updated: bfloat16 [4096, 4096], P('prow', 'pcol')
The draws below stay inside these ranges and needn't reach their ends.
Inputs may be any that keep to these rules, and one draw needn't show every extreme that they name: `pivots`: within one step the 256 pivot rows are distinct; their owners along the rows are uneven. `inverses`: each block is unit lower triangular.
All inputs are finite; a program needn't handle non-finite values.
Results may differ from the reference program's by a relative error of at most 0.0075.
Values may be sent and summed in bfloat16 or wider, within the bound.
No kernel may reach another device: no remote copies, remote signals or barrier semaphores. Data moves between devices by JAX's collectives and lax.ppermute only.
A program may use at most 64 MiB of HBM per device.

```python
import jax
import jax.numpy as jnp
from jax import lax

NB = 256
TILE = 128
STEPS = 4
ROW_DEV = 1024
ROWS = 4096
COLS = 4096
TILES = 32


def draw_inverses(key, part):
    key = jax.random.fold_in(key, 5)
    noise = jax.random.normal(key, (STEPS, NB, NB), jnp.float32)
    strict = jnp.tril(noise, -1) * (0.6 / NB ** 0.5)
    return (strict + jnp.eye(NB, dtype=jnp.float32)[None]).astype(jnp.bfloat16)


def draw_pivots(key, part):
    key = jax.random.fold_in(key, 7)
    row_ids = jnp.arange(ROWS, dtype=jnp.int32)
    owner = row_ids // ROW_DEV

    def one_step(sub):
        first, second, third = jax.random.split(sub, 3)
        weights = jax.random.randint(first, (ROWS // ROW_DEV,), 0, 4, dtype=jnp.int32)
        noise = jax.random.randint(second, (ROWS,), 0, 4096, dtype=jnp.int32)
        score = (weights[owner] * 4096 + noise) * ROWS + row_ids
        pinned = (row_ids == STEPS * NB) | (row_ids == ROWS - 1)
        score = jnp.where(pinned, 16384 * ROWS + row_ids, score)
        score = jnp.where(row_ids >= STEPS * NB, score, -1 - row_ids)
        picked = lax.top_k(score, NB)[1].astype(jnp.int32)
        return jax.random.permutation(third, picked).astype(jnp.int32)
    return jax.vmap(one_step)(jax.random.split(key, STEPS))


def touch_ends(entries, key, low, largest):
    index_at = [jax.random.randint(jax.random.fold_in(key, axis), (), 0, length) for axis, length in enumerate(entries.shape)]
    main_axis = entries.shape.index(max(entries.shape))
    neighbour = index_at[:main_axis] + [(index_at[main_axis] + 1) % entries.shape[main_axis]] + index_at[main_axis + 1:]
    return entries.at[tuple(index_at)].set(low).at[tuple(neighbour)].set(largest)


def block_levels(key, shape, cuts, smallest, top_value):
    gain = 1.0
    for axis_at, shards_of in cuts:
        draws = jax.random.uniform(jax.random.fold_in(jax.random.fold_in(key, 6), axis_at), (shards_of,), jnp.float32, smallest / len(cuts), top_value / len(cuts))
        gain = gain * jnp.repeat(jnp.exp(draws), shape[axis_at] // shards_of).reshape((-1,) + (1,) * (len(shape) - 1 - axis_at))
    return gain


def normal_values(stream_key, extent, deviation, reach, cuts=(), held_as=jnp.bfloat16):
    level = block_levels(stream_key, extent, cuts, -0.22, 0.18) if cuts else 1.0
    values = jax.random.normal(stream_key, extent, jnp.float32) * deviation * level
    return jnp.minimum(jnp.maximum(values, -reach), reach).astype(held_as)


def setup_inputs(seed: int = 0) -> dict:
    arg_keys = jax.random.split(jax.random.key(seed), 6)
    return {
        "matrix": normal_values(arg_keys[0], (ROWS, COLS), 1.0, 6.0, ((0, 4), (1, 8))),
        "panels": normal_values(arg_keys[1], (STEPS, NB, ROWS), NB ** -0.5, 0.375, ((1, 8), (2, 4))),
        "exponents": touch_ends(jax.random.randint(arg_keys[2], (STEPS, TILES), -3, 2), jax.random.fold_in(arg_keys[2], 1), -3, 1).astype(jnp.int32),
        "inverses": draw_inverses(jax.random.fold_in(arg_keys[5], 71), 0),
        "pivots": draw_pivots(jax.random.fold_in(arg_keys[5], 71), 0),
    }


def reference(matrix, panels, exponents, inverses, pivots):
    current = matrix
    row_ids = jnp.arange(ROWS, dtype=jnp.int32)
    for step in range(STEPS):
        top = step * NB
        chosen = current[pivots[step]]
        upper = current[top:top + NB]
        solved = jnp.dot(inverses[step], chosen, preferred_element_type=jnp.float32).astype(jnp.bfloat16)
        swapped = current.at[pivots[step]].set(upper)
        swapped = swapped.at[top:top + NB].set(solved)
        factor = jnp.repeat(jnp.exp2(exponents[step].astype(jnp.float32)), TILE).astype(jnp.bfloat16)
        lower = panels[step] * factor[None, :]
        lower_blocks = lower.reshape(NB, ROWS // ROW_DEV, ROW_DEV).transpose(1, 0, 2)
        swap_blocks = swapped.reshape(ROWS // ROW_DEV, ROW_DEV, COLS)

        def apply_block(pair):
            block_low, block_rows = pair
            change = lax.dot_general(block_low, solved, (((0,), (0,)), ((), ())), preferred_element_type=jnp.float32)
            return (block_rows.astype(jnp.float32) - change).astype(jnp.bfloat16)

        refreshed = lax.map(apply_block, (lower_blocks, swap_blocks)).reshape(ROWS, COLS)
        keep = row_ids >= top + NB
        current = jnp.where(keep[:, None], refreshed, swapped)
    return current
```

```python
import jax
import jax.numpy as jnp
from jax import lax
from jax.sharding import PartitionSpec as P

CHUNKS = ((0,), (1,), (2, 3))
BF = jnp.bfloat16
F32 = jnp.float32


def xor_pairs(size, mask):
    return [(i, i ^ mask) for i in range(size)]


def swap(value, axis, size, mask):
    return lax.ppermute(value, axis, xor_pairs(size, mask))


def gather_panels(own, size):
    if size != 8:
        me = lax.axis_index("pcol")
        whole = lax.all_gather(own, "pcol", axis=0)
        return [whole[me ^ m] for m in range(size)]
    x0 = swap(own, "pcol", 8, 1)
    z2 = swap(own, "pcol", 8, 4)
    z3 = swap(own, "pcol", 8, 6)
    z1 = swap(own, "pcol", 8, 2)
    z1x = swap(x0, "pcol", 8, 2)
    z2x = swap(z2, "pcol", 8, 1)
    z3x = swap(z3, "pcol", 8, 1)
    return [own, x0, z1, z1x, z2, z2x, z3, z3x]


def trade_rows(mine, here, row, rows_of_prow):
    n = mine.shape[0]
    if rows_of_prow != 4:
        chosen = lax.psum(jnp.where(row == 0, jnp.zeros_like(mine), mine), "prow")
        upper = lax.psum(jnp.where(row == 0, mine, jnp.zeros_like(mine)), "prow")
        return chosen.astype(F32).astype(BF), upper.astype(F32).astype(BF)
    other = swap(mine, "prow", 4, 1)
    low_chip = row < 2
    upper = jnp.where(row == 0, mine, other)
    picked = jnp.where(low_chip, jnp.where(row == 0, other, mine), mine + other)
    message = jnp.where(low_chip & ~here[:, None], upper, picked)
    core = row % 2
    half = n // 2
    first = jnp.where(core == 0, message[:half], message[half:])
    came = swap(first, "prow", 4, 2)
    rest = swap(came, "prow", 4, 1)
    low = jnp.where(core == 0, came, rest)
    high = jnp.where(core == 0, rest, came)
    came = jnp.concatenate([low, high])
    chosen = jnp.where(here[:, None], picked, came)
    upper = jnp.where(low_chip, upper, came)
    return chosen, upper


def make(n_row, n_col):
    def on_device(matrix, panels, exponents, inverses, pivots):
        row_dev = matrix.shape[0]
        steps, width = pivots.shape
        tile = row_dev // exponents.shape[1]
        part = width // n_col
        row = lax.axis_index("prow")
        me = lax.axis_index("pcol")
        first_row = row * row_dev
        local = jnp.arange(row_dev, dtype=jnp.int32)
        global_rows = first_row + local
        order = jnp.arange(n_col, dtype=jnp.int32) ^ me

        factor = jnp.repeat(jnp.exp2(exponents.astype(F32)), tile, axis=1).astype(BF)
        blocks = [None] * steps
        for chunk in CHUNKS:
            got = gather_panels(panels[chunk[0] : chunk[-1] + 1], n_col)
            for at, step in enumerate(chunk):
                blocks[step] = jnp.concatenate([g[at] for g in got]) * factor[step][None, :]
        current = matrix
        for step in range(steps):
            top = step * width
            root = top // row_dev
            assert root == 0
            local_piv = pivots[step] - first_row
            pick = (local_piv[:, None] == local[None, :]).astype(BF)
            here = (pivots[step] // (2 * row_dev)) == row // 2
            picked = jnp.dot(pick, current, preferred_element_type=F32).astype(BF)
            top_block = current[top : top + width]
            mine = jnp.where(row == 0, top_block, picked)
            chosen, upper = trade_rows(mine, here, row, n_row)
            solved = jnp.dot(inverses[step], chosen, preferred_element_type=F32).astype(BF)
            mixed = solved.reshape(n_col, part, -1)[order].reshape(width, -1)
            put = (global_rows[:, None] == pivots[step][None, :]).astype(BF)
            is_pivot = jnp.any(put > 0, axis=1)
            placed = jnp.dot(put, upper, preferred_element_type=F32)
            swapped = jnp.where(is_pivot[:, None], placed, current.astype(F32))
            change = lax.dot_general(blocks[step], mixed, (((0,), (0,)), ((), ())), preferred_element_type=F32)
            refreshed = (swapped - change).astype(BF)
            keep = global_rows >= top + width
            refreshed = jnp.where(keep[:, None], refreshed, current)
            in_top = row == 0
            top_rows = jnp.where(in_top, solved, refreshed[top : top + width])
            current = lax.dynamic_update_slice(refreshed, top_rows, (top, 0))
        return current

    return on_device


def solution(mesh):
    return jax.shard_map(
        make(mesh.shape["prow"], mesh.shape["pcol"]),
        mesh=mesh,
        in_specs=(P("prow", "pcol"), P(None, "pcol", "prow"), P(None, "prow"), P(), P()),
        out_specs=P("prow", "pcol"),
        check_vma=False,
    )
```

```python
import functools

import jax
import jax.numpy as jnp
from jax import lax
from jax.experimental import pallas as pl
from jax.experimental.pallas import tpu as pltpu
from jax.sharding import PartitionSpec as P

GROUPS = ((0,), (1, 2, 3))
CHUNKS = ((0,), (1, 2, 3))
BF = jnp.bfloat16
F32 = jnp.float32
I32 = jnp.int32
W = 256
VMEM = pl.BlockSpec(memory_space=pltpu.VMEM)
SMEM = pl.BlockSpec(memory_space=pltpu.SMEM)
FIRST, LOW, HIGH, IS_LOW, ROW, CORE, ME = range(7)


def group_pairs(steps):
    return [(k, e) for k in steps for e in steps if e < k]


PAIRS = [pair for steps in GROUPS for pair in group_pairs(steps)]
SPECIAL = len(CHUNKS) - 1


def swap(value, axis, size, mask):
    return lax.ppermute(value, axis, [(i, i ^ mask) for i in range(size)])


def dot_tn(a, b):
    return lax.dot_general(a, b, (((0,), (0,)), ((), ())), preferred_element_type=F32)


def dot_nt(a, b):
    return lax.dot_general(a, b, (((1,), (1,)), ((), ())), preferred_element_type=F32)


def dot(a, b):
    return jnp.dot(a, b, preferred_element_type=F32)


def pivot_views(piv_ref):
    rows = piv_ref[...]
    both = jnp.concatenate([rows, rows], axis=0)
    columns = jnp.transpose(both)
    return (lambda k: rows[k : k + 1, :]), (lambda k: columns[:, k : k + 1])


def matches(steps, row_of, col_of):
    out = {}
    for k in steps:
        found = jnp.zeros((W, 1), I32)
        terms = []
        for e in reversed([e for e in steps if e < k]):
            same = (col_of(k) == row_of(e)).astype(I32)
            same = same * (1 - found)
            terms.append((e, same.astype(F32).astype(BF)))
            found = found + jnp.sum(same, axis=1, keepdims=True)
        out[k] = (terms, found)
    return out


def later_matches(k, e, steps, row_of, col_of):
    found = jnp.zeros((1, W), I32)
    for q in steps:
        if e < q < k:
            found = jnp.maximum(found, jnp.max((col_of(q) == row_of(k)).astype(I32), axis=0, keepdims=True))
    return found


def scale_row(fac_ref, step, lo, count, tile):
    parts = [jnp.full((1, tile), fac_ref[step, t], F32) for t in range(lo // tile, (lo + count) // tile)]
    return jnp.concatenate(parts, axis=1) if len(parts) > 1 else parts[0]


def pick_rows(scal, col, source, row_dev):
    lane = lax.broadcasted_iota(I32, (W, row_dev), 1) + scal[FIRST]
    sel = (col == lane).astype(F32).astype(BF)
    return dot(sel, source)


def first_kernel(tile, scal, fac, piv, mat, pan, v_ref, sp_ref):
    row_dev = mat.shape[0]
    _, col_of = pivot_views(piv)
    is_top = scal[ROW] == 0
    if v_ref is not None:
        for at, k in enumerate(GROUPS[0]):
            got = pick_rows(scal, col_of(k), mat[...], row_dev)
            top = mat[k * W : (k + 1) * W, :].astype(F32)
            v_ref[at * W : (at + 1) * W, :] = jnp.where(is_top, top, got).astype(BF)
    if sp_ref is not None:
        lane = lax.broadcasted_iota(I32, (W, row_dev), 1) + scal[FIRST]
        scaled = {}
        for e in sorted({e for _, e in PAIRS}):
            scaled[e] = (pan[e].astype(F32) * scale_row(fac, e, 0, row_dev, tile)).astype(BF)
        sels = {k: (col_of(k) == lane).astype(F32).astype(BF) for k in sorted({k for k, _ in PAIRS})}
        for at, (k, e) in enumerate(PAIRS):
            got = dot_nt(scaled[e], sels[k])
            top = scaled[e][:, k * W : (k + 1) * W].astype(F32)
            sp_ref[:, at * W : (at + 1) * W] = jnp.where(is_top, top, got).astype(BF)


def slices_resolved(scal, piv, tops, picks):
    row_of, col_of = pivot_views(piv)
    out = []
    for steps in GROUPS:
        table = matches(steps, row_of, col_of)
        for k, e in group_pairs(steps):
            value = picks[(k, e)]
            between = [(q, m) for q, m in table[k][0] if q > e]
            if between:
                moved = sum(dot_nt(tops[(q, e)].astype(BF), m) for q, m in between)
                p = row_of(k)
                here = (p >= scal[LOW]) & (p < scal[HIGH])
                resolve = (later_matches(k, e, steps, row_of, col_of) > 0) & (here | (scal[IS_LOW] == 1))
                value = jnp.where(resolve, moved, value)
            out.append(value)
    return out


def here_lanes(scal, piv, k):
    p = piv[k : k + 1, :]
    return (p >= scal[LOW]) & (p < scal[HIGH])


def slice_message_kernel(scal, piv, own, other, out):
    is_top = scal[ROW] == 0
    low = scal[IS_LOW] == 1
    tops, picks, sums = {}, {}, {}
    for at, pair in enumerate(PAIRS):
        lanes = slice(at * W, (at + 1) * W)
        a, b = own[:, lanes].astype(F32), other[:, lanes].astype(F32)
        tops[pair] = jnp.where(is_top, a, b)
        picks[pair] = jnp.where(is_top, b, a)
        sums[pair] = a + b
    resolved = slices_resolved(scal, piv, tops, picks)
    for at, pair in enumerate(PAIRS):
        from_low = jnp.where(here_lanes(scal, piv, pair[0]), resolved[at], tops[pair])
        out[:, at * W : (at + 1) * W] = jnp.where(low, from_low, sums[pair]).astype(BF)


def slice_final_kernel(split, scal, piv, own, other, came, pan, out):
    is_top = scal[ROW] == 0
    low = scal[IS_LOW] == 1
    base = 0
    for k in CHUNKS[SPECIAL]:
        out[:, base : base + pan.shape[2]] = pan[k]
        base += pan.shape[2]
    tops, picks = {}, {}
    for at, pair in enumerate(PAIRS):
        lanes = slice(at * W, (at + 1) * W)
        a, b, c = own[:, lanes].astype(F32), other[:, lanes].astype(F32), came[:, lanes].astype(F32)
        tops[pair] = jnp.where(low, jnp.where(is_top, a, b), c)
        chip = jnp.where(low, jnp.where(is_top, b, a), a + b)
        picks[pair] = jnp.where(here_lanes(scal, piv, pair[0]), chip, c)
    resolved = slices_resolved(scal, piv, tops, picks)
    width = len(PAIRS) * W
    for at, pair in enumerate(PAIRS):
        if split:
            value = jnp.where(scal[CORE] == 0, tops[pair], resolved[at])
            out[:, base + at * W : base + (at + 1) * W] = value.astype(BF)
        else:
            out[:, base + at * W : base + (at + 1) * W] = tops[pair].astype(BF)
            out[:, base + width + at * W : base + width + (at + 1) * W] = resolved[at].astype(BF)


def rows_resolved(scal, steps, table, col_of, tops, picks):
    out = []
    for at, k in enumerate(steps):
        value = picks[at]
        terms, found = table[k]
        if terms:
            moved = sum(dot(m, tops[steps.index(e)].astype(BF)) for e, m in terms)
            p = col_of(k)
            here = (p >= scal[LOW]) & (p < scal[HIGH])
            value = jnp.where((found > 0) & (here | (scal[IS_LOW] == 1)), moved, value)
        out.append(value)
    return out


def here_column(scal, p):
    return (p >= scal[LOW]) & (p < scal[HIGH])


def row_message_kernel(steps, scal, piv, own, other, out):
    row_of, col_of = pivot_views(piv)
    n = len(steps)
    is_top = scal[ROW] == 0
    low = scal[IS_LOW] == 1
    a = [own[i * W : (i + 1) * W, :].astype(F32) for i in range(n)]
    b = [other[i * W : (i + 1) * W, :].astype(F32) for i in range(n)]
    tops = [jnp.where(is_top, x, y) for x, y in zip(a, b)]
    picks = [jnp.where(is_top, y, x) for x, y in zip(a, b)]
    table = matches(steps, row_of, col_of)
    resolved = rows_resolved(scal, steps, table, col_of, tops, picks)
    half = W // 2
    for i, k in enumerate(steps):
        from_low = jnp.where(here_column(scal, col_of(k)), resolved[i], tops[i])
        value = jnp.where(low, from_low, a[i] + b[i])
        out[i * half : (i + 1) * half, :] = jnp.where(scal[CORE] == 0, value[:half], value[half:]).astype(BF)


def step_kernel(steps, after, tile, n_piece, offsets, sp_at, split, *refs):
    pairs = group_pairs(steps)
    refs = list(refs)
    scal, fac, piv, own, other, came, rest, cur, inv = refs[:9]
    refs = refs[9:]
    chunk_ids = sorted({offsets[k][0] for k in steps})
    pieces = {}
    for c in chunk_ids:
        pieces[c] = refs[:n_piece]
        refs = refs[n_piece:]
    special = other_special = None
    if pairs:
        special = refs[:n_piece]
        refs = refs[n_piece:]
        if split:
            other_special = refs[0]
            refs = refs[1:]
    new = refs[0]
    refs = refs[1:]
    v_ref = None
    if after:
        v_ref = refs[0]
        refs = refs[1:]
    s_ref, mix_ref, u_ref = refs
    row_of, col_of = pivot_views(piv)
    n = len(steps)
    row_dev, columns = cur.shape
    part = W // n_piece
    is_top = scal[ROW] == 0
    low = scal[IS_LOW] == 1
    core0 = scal[CORE] == 0
    half = W // 2
    tops, picks = [], []
    for i, k in enumerate(steps):
        a = own[i * W : (i + 1) * W, :].astype(F32)
        b = other[i * W : (i + 1) * W, :].astype(F32)
        c = came[i * half : (i + 1) * half, :].astype(F32)
        d = rest[i * half : (i + 1) * half, :].astype(F32)
        got = jnp.concatenate([jnp.where(core0, c, d), jnp.where(core0, d, c)], axis=0)
        tops.append(jnp.where(low, jnp.where(is_top, a, b), got))
        chip = jnp.where(low, jnp.where(is_top, b, a), a + b)
        picks.append(jnp.where(here_column(scal, col_of(k)), chip, got))
    table = matches(steps, row_of, col_of)
    chosen = rows_resolved(scal, steps, table, col_of, tops, picks)

    def side_rows(pair, which):
        base = sp_at + PAIRS.index(pair) * W
        if not split:
            base = base + which * len(PAIRS) * W
            return jnp.concatenate([p[:, base : base + W] for p in special], axis=0)
        mine = jnp.concatenate([p[:, base : base + W] for p in special], axis=0)
        at = PAIRS.index(pair) * W
        theirs = other_special[:, at : at + W]
        mine_is = core0 if which == 0 else jnp.logical_not(core0)
        return jnp.where(mine_is, mine.astype(F32), theirs.astype(F32)).astype(BF)

    for i, k in enumerate(steps):
        acc, upper = chosen[i], tops[i]
        for j, e in enumerate(steps[:i]):
            mixed = mix_ref[j * W : (j + 1) * W, :]
            acc = acc - dot_tn(side_rows((k, e), 1), mixed)
            upper = upper - dot_tn(side_rows((k, e), 0), mixed)
        u_ref[i * W : (i + 1) * W, :] = upper.astype(BF)
        s_ref[i * W : (i + 1) * W, :] = dot(inv[k], acc.astype(BF)).astype(BF)
        for m in range(n_piece):
            if n_piece == 1:
                mix_ref[i * W : (i + 1) * W, :] = s_ref[i * W : (i + 1) * W, :]
                break
            start = pl.multiple_of((scal[ME] ^ m) * part, part)
            mix_ref[i * W + m * part : i * W + (m + 1) * part, :] = s_ref[pl.ds(i * W + start, part), :]

    for lo in range(0, row_dev, W):
        ids = lax.broadcasted_iota(I32, (W, W), 0) + scal[FIRST] + lo
        taken = jnp.zeros((W, 1), I32)
        placed = jnp.zeros((W, columns), F32)
        for i in reversed(range(n)):
            same = (ids == row_of(steps[i])).astype(I32) * (1 - taken)
            placed = placed + dot(same.astype(F32).astype(BF), u_ref[i * W : (i + 1) * W, :])
            taken = taken + jnp.sum(same, axis=1, keepdims=True)
        old = cur[lo : lo + W, :].astype(F32)
        acc = jnp.where(taken > 0, placed, old)
        lane = lax.broadcasted_iota(I32, (W, W), 1) + scal[FIRST] + lo
        alive = jnp.ones((1, W), F32)
        for i in reversed(range(n)):
            k = steps[i]
            c, off = offsets[k]
            block = jnp.concatenate([p[:, off + lo : off + lo + W] for p in pieces[c]], axis=0)
            weight = scale_row(fac, k, lo, W, tile) * alive
            block = (block.astype(F32) * weight).astype(BF)
            acc = acc - dot_tn(block, mix_ref[i * W : (i + 1) * W, :])
            if i:
                hit = jnp.max((col_of(k) == lane).astype(F32), axis=0, keepdims=True)
                alive = alive * (1.0 - hit)
        at = lo // W
        if at in steps:
            i = steps.index(at)
            acc = jnp.where(is_top, s_ref[i * W : (i + 1) * W, :].astype(F32), acc)
        elif at < steps[0]:
            acc = jnp.where(is_top, old, acc)
        new[lo : lo + W, :] = acc.astype(BF)
    for i, k in enumerate(after):
        got = pick_rows(scal, col_of(k), new[...], row_dev)
        top = new[k * W : (k + 1) * W, :].astype(F32)
        v_ref[i * W : (i + 1) * W, :] = jnp.where(is_top, top, got).astype(BF)


def call(kernel, shapes, n_smem, *args, scratch=()):
    single = not isinstance(shapes, (list, tuple))
    out = pl.pallas_call(
        kernel,
        out_shape=shapes,
        in_specs=[SMEM] * n_smem + [VMEM] * (len(args) - n_smem),
        out_specs=VMEM if single else [VMEM] * len(shapes),
        scratch_shapes=list(scratch),
        compiler_params=pltpu.CompilerParams(vmem_limit_bytes=40 * 1024 * 1024),
    )(*args)
    return out


def gather(own, n_col):
    if n_col != 8:
        return [lax.all_gather(own, "pcol", axis=0, tiled=True)]
    z2 = swap(own, "pcol", 8, 4)
    z3 = swap(own, "pcol", 8, 6)
    x0 = swap(own, "pcol", 8, 1)
    z1 = swap(own, "pcol", 8, 2)
    z1x = swap(x0, "pcol", 8, 2)
    z2x = swap(z2, "pcol", 8, 1)
    z3x = swap(z3, "pcol", 8, 1)
    return [own, x0, z1, z1x, z2, z2x, z3, z3x]


def make(n_row, n_col):
    split = n_row == 4
    n_piece = 8 if n_col == 8 else 1

    def psum_pair(own, row):
        zero = jnp.zeros_like(own)
        picks = lax.psum(jnp.where(row == 0, zero, own), "prow")
        tops = lax.psum(jnp.where(row == 0, own, zero), "prow")
        return picks.astype(F32).astype(BF), tops.astype(F32).astype(BF)

    def on_device(matrix, panels, exponents, inverses, pivots):
        row_dev, columns = matrix.shape
        steps_all = pivots.shape[0]
        assert steps_all * W <= row_dev and pivots.shape[1] == W
        tile = row_dev // exponents.shape[1]
        part = W // n_col
        row = lax.axis_index("prow")
        me = lax.axis_index("pcol")
        first_row = row * row_dev
        if split:
            chip = row // 2
            scal = jnp.stack([first_row, chip * 2 * row_dev, (chip + 1) * 2 * row_dev, (chip == 0).astype(I32), row, row % 2, me, me])
        else:
            zero = jnp.zeros((), I32)
            scal = jnp.stack([first_row, zero, zero + n_row * row_dev, zero + 1, row, zero, me, me])
        scal = scal.astype(I32)
        scal2 = scal if split else scal.at[ROW].set(1)
        top_scal = scal
        fac = jnp.exp2(exponents.astype(F32))

        wide = len(PAIRS) * W
        bf = lambda *shape: jax.ShapeDtypeStruct(shape, BF)

        def no_special(scal, fac, piv, mat, pan, v):
            first_kernel(tile, scal, fac, piv, mat, pan, v, None)

        def only_special(scal, fac, piv, mat, pan, sp):
            first_kernel(tile, scal, fac, piv, mat, pan, None, sp)

        arrived = [None] * len(CHUNKS)
        offsets = {}
        for c, chunk in enumerate(CHUNKS):
            for i, k in enumerate(chunk):
                offsets[k] = (c, i * row_dev)
        for c, chunk in enumerate(CHUNKS):
            if c != SPECIAL or not PAIRS:
                own = jnp.concatenate([panels[k] for k in chunk], axis=1)
                arrived[c] = gather(own, n_col)
        rows = call(no_special, bf(len(GROUPS[0]) * W, columns), 2, top_scal, fac, pivots, matrix, panels)
        sp_at = len(CHUNKS[SPECIAL]) * row_dev
        special = other_special = None
        if PAIRS:
            sp = call(only_special, bf(part, wide), 2, top_scal, fac, pivots, matrix, panels)
            if split:
                sp_other = swap(sp, "prow", 4, 1)
                message = call(slice_message_kernel, bf(part, wide), 1, scal, pivots, sp, sp_other)
                sp_came = swap(message, "prow", 4, 2)
            else:
                sp, sp_other = psum_pair(sp, row)
                sp_came = sp
            load = sp_at + (wide if split else 2 * wide)
            own = call(
                functools.partial(slice_final_kernel, split), bf(part, load), 1, scal2, pivots, sp, sp_other, sp_came, panels
            )
            arrived[SPECIAL] = gather(own, n_col)
            special = arrived[SPECIAL]
            if split:
                mine = jnp.concatenate([p[:, sp_at:] for p in special], axis=0)
                other_special = swap(mine, "prow", 4, 1)

        current = matrix
        for g, steps in enumerate(GROUPS):
            after = GROUPS[g + 1] if g + 1 < len(GROUPS) else ()
            n = len(steps)
            if split:
                other = swap(rows, "prow", 4, 1)
                message = call(functools.partial(row_message_kernel, steps), bf(n * W // 2, columns), 1, scal, pivots, rows, other)
                came = swap(message, "prow", 4, 2)
                rest = swap(came, "prow", 4, 1)
            else:
                rows, other = psum_pair(rows, row)
                came = rest = rows[: n * W // 2]
            pairs = group_pairs(steps)
            args = [scal2, fac, pivots, rows, other, came, rest, current, inverses]
            for c in sorted({offsets[k][0] for k in steps}):
                args += arrived[c]
            if pairs:
                args += special
                if split:
                    args.append(other_special)
            shapes = [bf(row_dev, columns)] + ([bf(len(after) * W, columns)] if after else [])
            out = call(
                functools.partial(step_kernel, steps, after, tile, n_piece, offsets, sp_at, split),
                shapes,
                2,
                *args,
                scratch=[pltpu.VMEM((n * W, columns), BF)] * 3,
            )
            current = out[0]
            rows = out[1] if after else None
        return current

    return on_device


def solution(mesh):
    return jax.shard_map(
        make(mesh.shape["prow"], mesh.shape["pcol"]),
        mesh=mesh,
        in_specs=(P("prow", "pcol"), P(None, "pcol", "prow"), P(None, "prow"), P(), P()),
        out_specs=P("prow", "pcol"),
        check_vma=False,
    )
```

```python
import functools

import jax
import jax.numpy as jnp
from jax import lax
from jax.experimental import pallas as pl
from jax.experimental.pallas import tpu as pltpu
from jax.sharding import PartitionSpec as P

STEPS = (0, 1, 2, 3)
PAIRS = [(k, e) for k in STEPS for e in STEPS if e < k]
BF = jnp.bfloat16
F32 = jnp.float32
I32 = jnp.int32
W = 256
VMEM = pl.BlockSpec(memory_space=pltpu.VMEM)
SMEM = pl.BlockSpec(memory_space=pltpu.SMEM)
COST = pl.CostEstimate(flops=20000000000, bytes_accessed=1000, transcendentals=0)
FIRST, LOW, HIGH, IS_LOW, ROW, CORE, ME = range(7)


def swap(value, axis, size, mask):
    return lax.ppermute(value, axis, [(i, i ^ mask) for i in range(size)])


def dot_tn(a, b):
    return lax.dot_general(a, b, (((0,), (0,)), ((), ())), preferred_element_type=F32)


def dot_nt(a, b):
    return lax.dot_general(a, b, (((1,), (1,)), ((), ())), preferred_element_type=F32)


def dot(a, b):
    return jnp.dot(a, b, preferred_element_type=F32)


def pivot_views(piv_ref):
    rows = piv_ref[...]
    both = jnp.concatenate([rows, rows], axis=0)
    columns = jnp.transpose(both)
    return (lambda k: rows[k : k + 1, :]), (lambda k: columns[:, k : k + 1])


def matches(steps, row_of, col_of):
    out = {}
    for k in steps:
        found = jnp.zeros((W, 1), I32)
        terms = []
        for e in reversed([e for e in steps if e < k]):
            same = (col_of(k) == row_of(e)).astype(I32)
            same = same * (1 - found)
            terms.append((e, same.astype(F32).astype(BF)))
            found = found + jnp.sum(same, axis=1, keepdims=True)
        out[k] = (terms, found)
    return out


def later_matches(k, e, steps, row_of, col_of):
    found = jnp.zeros((1, W), I32)
    for q in steps:
        if e < q < k:
            found = jnp.maximum(found, jnp.max((col_of(q) == row_of(k)).astype(I32), axis=0, keepdims=True))
    return found


def scale_row(exp_ref, step, lo, count, tile):
    parts = []
    for t in range(lo // tile, (lo + count) // tile):
        e = exp_ref[step, t]
        scale = jnp.where(e >= 0, jnp.where(e == 1, 2.0, 1.0), jnp.where(e == -1, 0.5, jnp.where(e == -2, 0.25, 0.125)))
        parts.append(jnp.full((1, tile), scale, F32))
    return jnp.concatenate(parts, axis=1) if len(parts) > 1 else parts[0]


def pick_rows(scal, col, source, row_dev):
    lane = lax.broadcasted_iota(I32, (W, row_dev), 1) + scal[FIRST]
    sel = (col == lane).astype(F32).astype(BF)
    return dot(sel, source)


def slice_pick_kernel(tile, scal, fac, piv, pan, sp_ref):
    row_dev = pan.shape[2]
    _, col_of = pivot_views(piv)
    is_top = scal[ROW] == 0
    lane = lax.broadcasted_iota(I32, (W, row_dev), 1) + scal[FIRST]
    for k in STEPS[1:]:
        sel = (col_of(k) == lane).astype(F32).astype(BF)
        scaled = jnp.concatenate([pan[e].astype(F32) * scale_row(fac, e, 0, row_dev, tile) for e in STEPS[:k]], axis=0).astype(BF)
        got = dot_nt(scaled, sel)
        top = scaled[:, k * W : (k + 1) * W].astype(F32)
        value = jnp.where(is_top, top, got).astype(BF)
        part = pan.shape[1]
        for e in STEPS[:k]:
            at = PAIRS.index((k, e))
            sp_ref[:, at * W : (at + 1) * W] = value[e * part : (e + 1) * part]


def row_pick_kernel(scal, piv, mat, v_ref):
    _, col_of = pivot_views(piv)
    is_top = scal[ROW] == 0
    for k in STEPS:
        @pl.when(is_top)
        def _():
            v_ref[k * W : (k + 1) * W, :] = mat[k * W : (k + 1) * W, :]

        @pl.when(jnp.logical_not(is_top))
        def _():
            v_ref[k * W : (k + 1) * W, :] = pick_rows(scal, col_of(k), mat[...], mat.shape[0]).astype(BF)


def pass_first(kernel, first, scal, *refs):
    kernel(first, scal, *refs)


def slices_resolved(scal, piv, tops, picks):
    row_of, col_of = pivot_views(piv)
    out = []
    table = matches(STEPS, row_of, col_of)
    for k, e in PAIRS:
        value = picks[(k, e)]
        between = [(q, m) for q, m in table[k][0] if q > e]
        if between:
            moved = sum(dot_nt(tops[(q, e)].astype(BF), m) for q, m in between)
            p = row_of(k)
            here = (p >= scal[LOW]) & (p < scal[HIGH])
            resolve = (later_matches(k, e, STEPS, row_of, col_of) > 0) & (here | (scal[IS_LOW] == 1))
            value = jnp.where(resolve, moved, value)
        out.append(value)
    return out


def here_lanes(scal, piv, k):
    p = piv[k : k + 1, :]
    return (p >= scal[LOW]) & (p < scal[HIGH])


def slice_message_kernel(scal, piv, own, other, out):
    is_top = scal[ROW] == 0
    low = scal[IS_LOW] == 1
    tops, picks, sums = {}, {}, {}
    for at, pair in enumerate(PAIRS):
        lanes = slice(at * W, (at + 1) * W)
        a, b = own[:, lanes].astype(F32), other[:, lanes].astype(F32)
        tops[pair] = jnp.where(is_top, a, b)
        picks[pair] = jnp.where(is_top, b, a)
        sums[pair] = a + b
    resolved = slices_resolved(scal, piv, tops, picks)
    for at, pair in enumerate(PAIRS):
        from_low = jnp.where(here_lanes(scal, piv, pair[0]), resolved[at], tops[pair])
        out[:, at * W : (at + 1) * W] = jnp.where(low, from_low, sums[pair]).astype(BF)


def slice_final_kernel(split, scal, piv, own, other, came, out):
    is_top = scal[ROW] == 0
    low = scal[IS_LOW] == 1
    tops, picks = {}, {}
    for at, pair in enumerate(PAIRS):
        lanes = slice(at * W, (at + 1) * W)
        a, b, c = own[:, lanes].astype(F32), other[:, lanes].astype(F32), came[:, lanes].astype(F32)
        tops[pair] = jnp.where(low, jnp.where(is_top, a, b), c)
        chip = jnp.where(low, jnp.where(is_top, b, a), a + b)
        picks[pair] = jnp.where(here_lanes(scal, piv, pair[0]), chip, c)
    resolved = slices_resolved(scal, piv, tops, picks)
    width = len(PAIRS) * W
    for at, pair in enumerate(PAIRS):
        if split:
            value = jnp.where(scal[CORE] == 0, tops[pair], resolved[at])
            out[:, at * W : (at + 1) * W] = value.astype(BF)
        else:
            out[:, at * W : (at + 1) * W] = tops[pair].astype(BF)
            out[:, width + at * W : width + (at + 1) * W] = resolved[at].astype(BF)


def rows_resolved(scal, steps, table, col_of, tops, picks):
    out = []
    for at, k in enumerate(steps):
        value = picks[at]
        terms, found = table[k]
        if terms:
            moved = sum(dot(m, tops[steps.index(e)].astype(BF)) for e, m in terms)
            p = col_of(k)
            here = (p >= scal[LOW]) & (p < scal[HIGH])
            value = jnp.where((found > 0) & (here | (scal[IS_LOW] == 1)), moved, value)
        out.append(value)
    return out


def here_column(scal, p):
    return (p >= scal[LOW]) & (p < scal[HIGH])


def row_message_kernel(scal, piv, own, other, out):
    steps = STEPS
    row_of, col_of = pivot_views(piv)
    n = len(steps)
    is_top = scal[ROW] == 0
    low = scal[IS_LOW] == 1
    a = [own[i * W : (i + 1) * W, :].astype(F32) for i in range(n)]
    b = [other[i * W : (i + 1) * W, :].astype(F32) for i in range(n)]
    tops = [jnp.where(is_top, x, y) for x, y in zip(a, b)]
    picks = [jnp.where(is_top, y, x) for x, y in zip(a, b)]
    table = matches(steps, row_of, col_of)
    resolved = rows_resolved(scal, steps, table, col_of, tops, picks)
    half = W // 2
    for i, k in enumerate(steps):
        from_low = jnp.where(here_column(scal, col_of(k)), resolved[i], tops[i])
        value = jnp.where(low, from_low, a[i] + b[i])
        out[i * half : (i + 1) * half, :] = jnp.where(scal[CORE] == 0, value[:half], value[half:]).astype(BF)


def chain_kernel(tile, n_piece, split, scal, *refs):
    fac, piv, own, other, came, rest, cur, inv = refs[:8]
    special = refs[8 : 8 + n_piece]
    refs = refs[8 + n_piece :]
    other_special = None
    if split:
        other_special = refs[0]
        refs = refs[1:]
    mix_ref, base_ref, weight_ref, s_ref, u_ref = refs
    row_of, col_of = pivot_views(piv)
    row_dev, columns = cur.shape
    part = W // n_piece
    is_top = scal[ROW] == 0
    top_block = scal[FIRST] == 0
    low = scal[IS_LOW] == 1
    core0 = scal[CORE] == 0
    half = W // 2
    tops, picks = [], []
    for k in STEPS:
        a = own[k * W : (k + 1) * W, :].astype(F32)
        b = other[k * W : (k + 1) * W, :].astype(F32)
        c = came[k * half : (k + 1) * half, :].astype(F32)
        d = rest[k * half : (k + 1) * half, :].astype(F32)
        got = jnp.concatenate([jnp.where(core0, c, d), jnp.where(core0, d, c)], axis=0)
        tops.append(jnp.where(low, jnp.where(is_top, a, b), got))
        chip = jnp.where(low, jnp.where(is_top, b, a), a + b)
        picks.append(jnp.where(here_column(scal, col_of(k)), chip, got))
    table = matches(STEPS, row_of, col_of)
    chosen = rows_resolved(scal, STEPS, table, col_of, tops, picks)

    def side_rows(pair, which):
        base = PAIRS.index(pair) * W
        if not split:
            base = base + which * len(PAIRS) * W
            return jnp.concatenate([p[:, base : base + W] for p in special], axis=0)
        mine = jnp.concatenate([p[:, base : base + W] for p in special], axis=0)
        theirs = other_special[:, base : base + W]
        mine_is = core0 if which == 0 else jnp.logical_not(core0)
        return jnp.where(mine_is, mine.astype(F32), theirs.astype(F32)).astype(BF)

    for k in STEPS:
        acc, upper = chosen[k], tops[k]
        for e in STEPS[:k]:
            mixed = mix_ref[e * W : (e + 1) * W, :]
            acc = acc - dot_tn(side_rows((k, e), 1), mixed)
            upper = upper - dot_tn(side_rows((k, e), 0), mixed)
        u_ref[k * W : (k + 1) * W, :] = upper.astype(BF)
        s_ref[k * W : (k + 1) * W, :] = dot(inv[k], acc.astype(BF)).astype(BF)
        for m in range(n_piece):
            if n_piece == 1:
                mix_ref[k * W : (k + 1) * W, :] = s_ref[k * W : (k + 1) * W, :]
                break
            start = pl.multiple_of((scal[ME] ^ m) * part, part)
            mix_ref[k * W + m * part : k * W + (m + 1) * part, :] = s_ref[pl.ds(k * W + start, part), :]

    for lo in range(0, row_dev, W):
        ids = lax.broadcasted_iota(I32, (W, W), 0) + scal[FIRST] + lo
        lane = lax.broadcasted_iota(I32, (W, W), 1) + scal[FIRST] + lo
        taken = jnp.zeros((W, 1), I32)
        placed = jnp.zeros((W, columns), F32)
        alive = jnp.where(top_block, jnp.zeros((1, W), F32), jnp.ones((1, W), F32))
        for k in reversed(STEPS):
            same = (ids == row_of(k)).astype(I32) * (1 - taken)
            placed = placed + dot(same.astype(F32).astype(BF), u_ref[k * W : (k + 1) * W, :])
            taken = taken + jnp.sum(same, axis=1, keepdims=True)
            weight_ref[k : k + 1, lo : lo + W] = scale_row(fac, k, lo, W, tile) * alive
            if k:
                hit = jnp.max((col_of(k) == lane).astype(F32), axis=0, keepdims=True)
                alive = alive * (1.0 - hit)
        value = jnp.where(taken > 0, placed, cur[lo : lo + W, :].astype(F32))
        value = jnp.where(top_block, s_ref[lo : lo + W, :].astype(F32), value)
        base_ref[lo : lo + W, :] = value.astype(BF)


def update_kernel(n_piece, base, weight, mix, *refs):
    pieces, out = refs[:n_piece], refs[n_piece]
    acc = base[...].astype(F32)
    for k in STEPS:
        block = jnp.concatenate([p[k] for p in pieces], axis=0).astype(F32)
        block = (block * weight[k : k + 1, :]).astype(BF)
        acc = acc - dot_tn(block, mix[k * W : (k + 1) * W, :])
    out[...] = acc.astype(BF)


def place(split, row_dev, n_row, summed):
    row = lax.axis_index("prow")
    me = lax.axis_index("pcol")
    first = row * row_dev
    if split:
        chip = row // 2
        return [first, chip * 2 * row_dev, (chip + 1) * 2 * row_dev, (chip == 0).astype(I32), row, row % 2, me]
    return [first, 0, n_row * row_dev, 1, 1 if summed else row, 0, me]


def call(kernel, where, shapes, n_smem, *args, scratch=()):
    single = not isinstance(shapes, (list, tuple))

    def body(*refs):
        kernel(place(*where), *refs)

    return pl.pallas_call(
        body,
        out_shape=shapes,
        in_specs=[SMEM] * n_smem + [VMEM] * (len(args) - n_smem),
        out_specs=VMEM if single else [VMEM] * len(shapes),
        scratch_shapes=list(scratch),
        cost_estimate=COST,
        compiler_params=pltpu.CompilerParams(vmem_limit_bytes=40 * 1024 * 1024),
    )(*args)


def gather(own, axis):
    return [lax.all_gather(own, "pcol", axis=axis, tiled=True)]


def after(value, *others):
    return lax.optimization_barrier((value,) + others)[0]


def make(n_row, n_col):
    split = n_row == 4 and n_col == 8
    n_piece = 8 if split else 1

    def psum_pair(own, row):
        zero = jnp.zeros_like(own)
        picks = lax.psum(jnp.where(row == 0, zero, own), "prow")
        tops = lax.psum(jnp.where(row == 0, own, zero), "prow")
        return picks.astype(F32).astype(BF), tops.astype(F32).astype(BF)

    def on_device(matrix, panels, exponents, inverses, pivots):
        row_dev, columns = matrix.shape
        assert len(STEPS) * W == row_dev and pivots.shape == (len(STEPS), W)
        tile = row_dev // exponents.shape[1]
        part = W // n_col
        row = lax.axis_index("prow")
        where = (split, row_dev, n_row, False)
        where2 = (split, row_dev, n_row, True)
        wide = len(PAIRS) * W
        bf = lambda *shape: jax.ShapeDtypeStruct(shape, BF)

        sp = call(functools.partial(pass_first, slice_pick_kernel, tile), where, bf(part, wide), 1, exponents, pivots, panels)
        rows = call(row_pick_kernel, where, bf(row_dev, columns), 0, pivots, matrix)
        load = wide if split else 2 * wide
        final_slices = functools.partial(pass_first, slice_final_kernel, split)
        if split:
            sp_other = swap(sp, "prow", 4, 1)
            message = call(slice_message_kernel, where, bf(part, wide), 0, pivots, sp, sp_other)
            sp_came = swap(message, "prow", 4, 2)
        else:
            sp, sp_other = psum_pair(sp, row)
            sp_came = sp
        if n_piece == 8:
            bz2 = swap(panels, "pcol", 8, 4)
            bx0 = swap(panels, "pcol", 8, 1)
            bz1 = swap(panels, "pcol", 8, 2)
            sp_came = after(sp_came, bx0, bz1)
            own = call(final_slices, where2, bf(part, load), 0, pivots, sp, sp_other, sp_came)
        else:
            own = call(final_slices, where2, bf(part, load), 0, pivots, sp, sp_other, sp_came)
            bulk, special = gather(panels, 1), gather(own, 0)
        if split:
            other = swap(rows, "prow", 4, 1)
            message = call(row_message_kernel, where, bf(row_dev // 2, columns), 0, after(pivots, own), rows, other)
            came = swap(message, "prow", 4, 2)
            rest = None
        else:
            message = rows
            rows, other = psum_pair(rows, row)
            came = rest = rows[: row_dev // 2]
        held = pivots
        if n_piece == 8:
            sz2 = swap(own, "pcol", 8, 4)
            sz3 = swap(own, "pcol", 8, 6)
            sx0 = swap(own, "pcol", 8, 1)
            sz1 = swap(after(own, message), "pcol", 8, 2)
            sz1x = swap(after(sx0, message), "pcol", 8, 2)
            bz1x = swap(after(bx0, sx0), "pcol", 8, 2)
            bz3 = swap(after(panels, bz2), "pcol", 8, 6)
            sz2x = swap(after(sz2, bz2, message), "pcol", 8, 1)
            sz3x = swap(sz3, "pcol", 8, 1)
            bz2x = swap(after(bz2, sz3), "pcol", 8, 1)
            bz3x = swap(bz3, "pcol", 8, 1)
            bulk = [panels, bx0, bz1, bz1x, bz2, bz2x, bz3, bz3x]
            special = [own, sx0, sz1, sz1x, sz2, sz2x, sz3, sz3x]
            rest = swap(after(came, bz3), "prow", 4, 1)
            special = list(after(tuple(special), bz1x, bz2x))
        if split:
            mine = jnp.concatenate(special, axis=0)
            special = special + [swap(mine, "prow", 4, 1)]
        mix, base, weight = call(
            functools.partial(chain_kernel, tile, n_piece, split),
            where2,
            [bf(row_dev, columns), bf(row_dev, columns), jax.ShapeDtypeStruct((8, row_dev), F32)],
            1,
            exponents, held, rows, other, came, rest, matrix, inverses, *special,
            scratch=[pltpu.VMEM((row_dev, columns), BF)] * 2,
        )
        return pl.pallas_call(
            functools.partial(update_kernel, n_piece),
            out_shape=bf(row_dev, columns),
            grid=(row_dev // W,),
            in_specs=[
                pl.BlockSpec((W, columns), lambda i: (i, 0)),
                pl.BlockSpec((8, W), lambda i: (0, i)),
                pl.BlockSpec((row_dev, columns), lambda i: (0, 0)),
            ]
            + [pl.BlockSpec((len(STEPS), W // n_piece, W), lambda i: (0, 0, i))] * n_piece,
            out_specs=pl.BlockSpec((W, columns), lambda i: (i, 0)),
            cost_estimate=COST,
            compiler_params=pltpu.CompilerParams(vmem_limit_bytes=40 * 1024 * 1024),
        )(base, weight, mix, *bulk)

    return on_device


def solution(mesh):
    return jax.shard_map(
        make(mesh.shape["prow"], mesh.shape["pcol"]),
        mesh=mesh,
        in_specs=(P("prow", "pcol"), P(None, "pcol", "prow"), P(None, "prow"), P(), P()),
        out_specs=P("prow", "pcol"),
        check_vma=False,
    )
```

```python
import functools

import jax
import jax.numpy as jnp
from jax import lax
from jax.experimental import pallas as pl
from jax.experimental.pallas import tpu as pltpu
from jax.sharding import PartitionSpec as P

STEPS = (0, 1, 2, 3)
PAIRS = [(k, e) for k in STEPS for e in STEPS if e < k]
BF = jnp.bfloat16
F32 = jnp.float32
I32 = jnp.int32
W = 256
VMEM = pl.BlockSpec(memory_space=pltpu.VMEM)
SMEM = pl.BlockSpec(memory_space=pltpu.SMEM)
COST = pl.CostEstimate(flops=1000, bytes_accessed=1000, transcendentals=0)
FIRST, LOW, HIGH, IS_LOW, ROW, CORE, ME = range(7)


def swap(value, axis, size, mask):
    return lax.ppermute(value, axis, [(i, i ^ mask) for i in range(size)])


def dot_tn(a, b):
    return lax.dot_general(a, b, (((0,), (0,)), ((), ())), preferred_element_type=F32)


def dot_nt(a, b):
    return lax.dot_general(a, b, (((1,), (1,)), ((), ())), preferred_element_type=F32)


def dot(a, b):
    return jnp.dot(a, b, preferred_element_type=F32)


def pivot_views(piv_ref):
    rows = piv_ref[...]
    both = jnp.concatenate([rows, rows], axis=0)
    columns = jnp.transpose(both)
    return (lambda k: rows[k : k + 1, :]), (lambda k: columns[:, k : k + 1])


def matches(steps, row_of, col_of):
    out = {}
    for k in steps:
        found = jnp.zeros((W, 1), I32)
        terms = []
        for e in reversed([e for e in steps if e < k]):
            same = (col_of(k) == row_of(e)).astype(I32)
            same = same * (1 - found)
            terms.append((e, same.astype(F32).astype(BF)))
            found = found + jnp.sum(same, axis=1, keepdims=True)
        out[k] = (terms, found)
    return out


def later_matches(k, e, steps, row_of, col_of):
    found = jnp.zeros((1, W), I32)
    for q in steps:
        if e < q < k:
            found = jnp.maximum(found, jnp.max((col_of(q) == row_of(k)).astype(I32), axis=0, keepdims=True))
    return found


def scale_row(exp_ref, step, lo, count, tile):
    parts = []
    for t in range(lo // tile, (lo + count) // tile):
        e = exp_ref[step, t]
        scale = jnp.where(e >= 0, jnp.where(e == 1, 2.0, 1.0), jnp.where(e == -1, 0.5, jnp.where(e == -2, 0.25, 0.125)))
        parts.append(jnp.full((1, tile), scale, F32))
    return jnp.concatenate(parts, axis=1) if len(parts) > 1 else parts[0]


def pick_rows(scal, col, source, row_dev):
    lane = lax.broadcasted_iota(I32, (W, row_dev), 1) + scal[FIRST]
    sel = (col == lane).astype(F32).astype(BF)
    return dot(sel, source)


def slice_pick_kernel(tile, scal, fac, piv, pan, sp_ref):
    row_dev = pan.shape[2]
    _, col_of = pivot_views(piv)
    is_top = scal[ROW] == 0
    lane = lax.broadcasted_iota(I32, (W, row_dev), 1) + scal[FIRST]
    for k in STEPS[1:]:
        sel = (col_of(k) == lane).astype(F32).astype(BF)
        scaled = jnp.concatenate([pan[e].astype(F32) * scale_row(fac, e, 0, row_dev, tile) for e in STEPS[:k]], axis=0).astype(BF)
        got = dot_nt(scaled, sel)
        top = scaled[:, k * W : (k + 1) * W].astype(F32)
        value = jnp.where(is_top, top, got).astype(BF)
        part = pan.shape[1]
        for e in STEPS[:k]:
            at = PAIRS.index((k, e))
            sp_ref[:, at * W : (at + 1) * W] = value[e * part : (e + 1) * part]


def row_pick_kernel(scal, piv, mat, v_ref):
    _, col_of = pivot_views(piv)
    is_top = scal[ROW] == 0
    for k in STEPS:
        @pl.when(is_top)
        def _():
            v_ref[k * W : (k + 1) * W, :] = mat[k * W : (k + 1) * W, :]

        @pl.when(jnp.logical_not(is_top))
        def _():
            v_ref[k * W : (k + 1) * W, :] = pick_rows(scal, col_of(k), mat[...], mat.shape[0]).astype(BF)


def pass_first(kernel, first, scal, *refs):
    kernel(first, scal, *refs)


def slices_resolved(scal, piv, tops, picks):
    row_of, col_of = pivot_views(piv)
    out = []
    table = matches(STEPS, row_of, col_of)
    for k, e in PAIRS:
        value = picks[(k, e)]
        between = [(q, m) for q, m in table[k][0] if q > e]
        if between:
            moved = sum(dot_nt(tops[(q, e)].astype(BF), m) for q, m in between)
            p = row_of(k)
            here = (p >= scal[LOW]) & (p < scal[HIGH])
            resolve = (later_matches(k, e, STEPS, row_of, col_of) > 0) & (here | (scal[IS_LOW] == 1))
            value = jnp.where(resolve, moved, value)
        out.append(value)
    return out


def here_lanes(scal, piv, k):
    p = piv[k : k + 1, :]
    return (p >= scal[LOW]) & (p < scal[HIGH])


def slice_message_kernel(scal, piv, own, other, out):
    is_top = scal[ROW] == 0
    low = scal[IS_LOW] == 1
    tops, picks, sums = {}, {}, {}
    for at, pair in enumerate(PAIRS):
        lanes = slice(at * W, (at + 1) * W)
        a, b = own[:, lanes].astype(F32), other[:, lanes].astype(F32)
        tops[pair] = jnp.where(is_top, a, b)
        picks[pair] = jnp.where(is_top, b, a)
        sums[pair] = a + b
    resolved = slices_resolved(scal, piv, tops, picks)
    for at, pair in enumerate(PAIRS):
        from_low = jnp.where(here_lanes(scal, piv, pair[0]), resolved[at], tops[pair])
        out[:, at * W : (at + 1) * W] = jnp.where(low, from_low, sums[pair]).astype(BF)


def slice_final_kernel(split, scal, piv, own, other, came, out):
    is_top = scal[ROW] == 0
    low = scal[IS_LOW] == 1
    tops, picks = {}, {}
    for at, pair in enumerate(PAIRS):
        lanes = slice(at * W, (at + 1) * W)
        a, b, c = own[:, lanes].astype(F32), other[:, lanes].astype(F32), came[:, lanes].astype(F32)
        tops[pair] = jnp.where(low, jnp.where(is_top, a, b), c)
        chip = jnp.where(low, jnp.where(is_top, b, a), a + b)
        picks[pair] = jnp.where(here_lanes(scal, piv, pair[0]), chip, c)
    resolved = slices_resolved(scal, piv, tops, picks)
    width = len(PAIRS) * W
    for at, pair in enumerate(PAIRS):
        if split:
            value = jnp.where(scal[CORE] == 0, tops[pair], resolved[at])
            out[:, at * W : (at + 1) * W] = value.astype(BF)
        else:
            out[:, at * W : (at + 1) * W] = tops[pair].astype(BF)
            out[:, width + at * W : width + (at + 1) * W] = resolved[at].astype(BF)


def rows_resolved(scal, steps, table, col_of, tops, picks):
    out = []
    for at, k in enumerate(steps):
        value = picks[at]
        terms, found = table[k]
        if terms:
            moved = sum(dot(m, tops[steps.index(e)].astype(BF)) for e, m in terms)
            p = col_of(k)
            here = (p >= scal[LOW]) & (p < scal[HIGH])
            value = jnp.where((found > 0) & (here | (scal[IS_LOW] == 1)), moved, value)
        out.append(value)
    return out


def here_column(scal, p):
    return (p >= scal[LOW]) & (p < scal[HIGH])


def row_message_kernel(scal, piv, own, other, out):
    steps = STEPS
    row_of, col_of = pivot_views(piv)
    n = len(steps)
    is_top = scal[ROW] == 0
    low = scal[IS_LOW] == 1
    a = [own[i * W : (i + 1) * W, :].astype(F32) for i in range(n)]
    b = [other[i * W : (i + 1) * W, :].astype(F32) for i in range(n)]
    tops = [jnp.where(is_top, x, y) for x, y in zip(a, b)]
    picks = [jnp.where(is_top, y, x) for x, y in zip(a, b)]
    table = matches(steps, row_of, col_of)
    resolved = rows_resolved(scal, steps, table, col_of, tops, picks)
    half = W // 2
    for i, k in enumerate(steps):
        from_low = jnp.where(here_column(scal, col_of(k)), resolved[i], tops[i])
        value = jnp.where(low, from_low, a[i] + b[i])
        out[i * half : (i + 1) * half, :] = jnp.where(scal[CORE] == 0, value[:half], value[half:]).astype(BF)


def prepare_kernel(tile, scal, exps, piv, cur, put_ref, base_ref, weight_ref):
    row_of, col_of = pivot_views(piv)
    row_dev, columns = cur.shape
    top_block = scal[FIRST] == 0
    for lo in range(0, row_dev, W):
        ids = lax.broadcasted_iota(I32, (W, W), 0) + scal[FIRST] + lo
        lane = lax.broadcasted_iota(I32, (W, W), 1) + scal[FIRST] + lo
        taken = jnp.zeros((W, 1), I32)
        alive = jnp.where(top_block, jnp.zeros((1, W), F32), jnp.ones((1, W), F32))
        for k in reversed(STEPS):
            same = (ids == row_of(k)).astype(I32) * (1 - taken)
            put_ref[lo : lo + W, k * W : (k + 1) * W] = same.astype(F32).astype(BF)
            taken = taken + jnp.sum(same, axis=1, keepdims=True)
            weight_ref[k : k + 1, lo : lo + W] = scale_row(exps, k, lo, W, tile) * alive
            if k:
                hit = jnp.max((col_of(k) == lane).astype(F32), axis=0, keepdims=True)
                alive = alive * (1.0 - hit)
        base_ref[lo : lo + W, :] = jnp.where(taken > 0, 0.0, cur[lo : lo + W, :].astype(F32)).astype(BF)


def chain_kernel(n_piece, split, n_side, scal, *refs):
    piv, own, other, came, rest, put, start_rows, inv = refs[:8]
    sides = refs[8 : 8 + n_side]
    refs = refs[8 + n_side :]
    mix_ref, base_ref, s_ref, u_ref = refs
    row_of, col_of = pivot_views(piv)
    row_dev, columns = start_rows.shape
    part = W // n_piece
    is_top = scal[ROW] == 0
    top_block = scal[FIRST] == 0
    low = scal[IS_LOW] == 1
    core0 = scal[CORE] == 0
    half = W // 2
    tops, picks = [], []
    for k in STEPS:
        a = own[k * W : (k + 1) * W, :].astype(F32)
        b = other[k * W : (k + 1) * W, :].astype(F32)
        c = came[k * half : (k + 1) * half, :].astype(F32)
        d = rest[k * half : (k + 1) * half, :].astype(F32)
        got = jnp.concatenate([jnp.where(core0, c, d), jnp.where(core0, d, c)], axis=0)
        tops.append(jnp.where(low, jnp.where(is_top, a, b), got))
        chip = jnp.where(low, jnp.where(is_top, b, a), a + b)
        picks.append(jnp.where(here_column(scal, col_of(k)), chip, got))
    table = matches(STEPS, row_of, col_of)
    chosen = rows_resolved(scal, STEPS, table, col_of, tops, picks)

    def panel_rows(arrays, base):
        if len(arrays) == 1:
            return arrays[0][:, base : base + W]
        line, cross = arrays
        blocks = []
        for z in range(n_piece // 2):
            blocks += [line[z * part : (z + 1) * part, base : base + W], cross[z * part : (z + 1) * part, base : base + W]]
        return jnp.concatenate(blocks, axis=0)

    def side_rows(pair, which):
        base = PAIRS.index(pair) * W
        if not split:
            return panel_rows(sides, base + which * len(PAIRS) * W)
        mine = panel_rows(sides[: n_side // 2], base)
        theirs = panel_rows(sides[n_side // 2 :], base)
        mine_is = core0 if which == 0 else jnp.logical_not(core0)
        return jnp.where(mine_is, mine.astype(F32), theirs.astype(F32)).astype(BF)

    for k in STEPS:
        acc, upper = chosen[k], tops[k]
        for e in STEPS[:k]:
            mixed = mix_ref[e * W : (e + 1) * W, :]
            acc = acc - dot_tn(side_rows((k, e), 1), mixed)
            upper = upper - dot_tn(side_rows((k, e), 0), mixed)
        u_ref[k * W : (k + 1) * W, :] = upper.astype(BF)
        s_ref[k * W : (k + 1) * W, :] = dot(inv[k], acc.astype(BF)).astype(BF)
        for m in range(n_piece):
            if n_piece == 1:
                mix_ref[k * W : (k + 1) * W, :] = s_ref[k * W : (k + 1) * W, :]
                break
            start = pl.multiple_of((scal[ME] ^ m) * part, part)
            mix_ref[k * W + m * part : k * W + (m + 1) * part, :] = s_ref[pl.ds(k * W + start, part), :]

    @pl.when(top_block)
    def _():
        base_ref[...] = s_ref[...]

    @pl.when(jnp.logical_not(top_block))
    def _():
        for lo in range(0, row_dev, W):
            placed = dot(put[lo : lo + W, :], u_ref[...])
            base_ref[lo : lo + W, :] = (start_rows[lo : lo + W, :].astype(F32) + placed).astype(BF)


def update_kernel(n_piece, base, weight, mix, *refs):
    pieces, out = refs[:n_piece], refs[n_piece]
    acc = base[...].astype(F32)
    for k in STEPS:
        block = jnp.concatenate([p[k] for p in pieces], axis=0) * weight[k : k + 1, :].astype(BF)
        acc = acc - dot_tn(block, mix[k * W : (k + 1) * W, :])
    out[...] = acc.astype(BF)


def place(split, row_dev, n_row, summed):
    row = lax.axis_index("prow")
    me = lax.axis_index("pcol")
    first = row * row_dev
    if split:
        chip = row // 2
        return [first, chip * 2 * row_dev, (chip + 1) * 2 * row_dev, (chip == 0).astype(I32), row, row % 2, me]
    return [first, 0, n_row * row_dev, 1, 1 if summed else row, 0, me]


def call(kernel, where, shapes, n_smem, *args, scratch=()):
    single = not isinstance(shapes, (list, tuple))

    def body(*refs):
        kernel(place(*where), *refs)

    return pl.pallas_call(
        body,
        out_shape=shapes,
        in_specs=[SMEM] * n_smem + [VMEM] * (len(args) - n_smem),
        out_specs=VMEM if single else [VMEM] * len(shapes),
        scratch_shapes=list(scratch),
        cost_estimate=COST,
        compiler_params=pltpu.CompilerParams(vmem_limit_bytes=40 * 1024 * 1024),
    )(*args)


def gather(own, axis):
    return [lax.all_gather(own, "pcol", axis=axis, tiled=True)]


def after(value, *others):
    return lax.optimization_barrier((value,) + others)[0]


def make(n_row, n_col):
    split = n_row == 4 and n_col == 8
    n_piece = 8 if split else 1

    def psum_pair(own, row):
        zero = jnp.zeros_like(own)
        picks = lax.psum(jnp.where(row == 0, zero, own), "prow")
        tops = lax.psum(jnp.where(row == 0, own, zero), "prow")
        return picks.astype(F32).astype(BF), tops.astype(F32).astype(BF)

    def on_device(matrix, panels, exponents, inverses, pivots):
        row_dev, columns = matrix.shape
        assert len(STEPS) * W == row_dev and pivots.shape == (len(STEPS), W)
        tile = row_dev // exponents.shape[1]
        part = W // n_col
        row = lax.axis_index("prow")
        where = (split, row_dev, n_row, False)
        where2 = (split, row_dev, n_row, True)
        wide = len(PAIRS) * W
        bf = lambda *shape: jax.ShapeDtypeStruct(shape, BF)

        sp = call(functools.partial(pass_first, slice_pick_kernel, tile), where, bf(part, wide), 1, exponents, pivots, panels)
        rows = call(row_pick_kernel, where, bf(row_dev, columns), 0, pivots, matrix)
        load = wide if split else 2 * wide
        final_slices = functools.partial(pass_first, slice_final_kernel, split)
        if split:
            sp_other = swap(sp, "prow", 4, 1)
            message = call(slice_message_kernel, where, bf(part, wide), 0, pivots, sp, sp_other)
            sp_came = swap(message, "prow", 4, 2)
        else:
            sp, sp_other = psum_pair(sp, row)
            sp_came = sp
        if n_piece == 8:
            bz2 = swap(panels, "pcol", 8, 4)
            bx0 = swap(panels, "pcol", 8, 1)
            bz1 = swap(panels, "pcol", 8, 2)
            sp_came = after(sp_came, bx0)
            own = call(final_slices, where2, bf(part, load), 0, pivots, sp, sp_other, sp_came)
        else:
            own = call(final_slices, where2, bf(part, load), 0, pivots, sp, sp_other, sp_came)
            bulk, special = gather(panels, 1), gather(own, 0)
        if split:
            other = swap(rows, "prow", 4, 1)
            message = call(row_message_kernel, where, bf(row_dev // 2, columns), 0, after(pivots, own), rows, other)
            came = swap(message, "prow", 4, 2)
            rest = None
        else:
            message = rows
            rows, other = psum_pair(rows, row)
            came = rest = rows[: row_dev // 2]
        held = pivots
        put, start_rows, weight = call(
            functools.partial(pass_first, prepare_kernel, tile),
            where,
            [bf(row_dev, row_dev), bf(row_dev, columns), jax.ShapeDtypeStruct((8, row_dev), F32)],
            1,
            exponents, after(pivots, message), matrix,
        )
        if n_piece == 8:
            sz2 = swap(after(own, message, bz1), "pcol", 8, 4)
            sz3 = swap(own, "pcol", 8, 6)
            sz1 = swap(own, "pcol", 8, 2)
            bz3 = swap(after(panels, bz2, weight), "pcol", 8, 6)
            line = jnp.concatenate([own, sz1, sz2, sz3], axis=0)
            cross = swap(line, "pcol", 8, 1)
            bz2x = swap(after(bz2, sz3), "pcol", 8, 1)
            bz3x = swap(bz3, "pcol", 8, 1)
            line_other = swap(line, "prow", 4, 1)
            bz1x = swap(after(bx0, line_other), "pcol", 8, 2)
            rest = swap(after(came, bz3, bz2x), "prow", 4, 1)
            bulk = [panels, bx0, bz1, bz1x, bz2, bz2x, bz3, bz3x]
            cross_other = swap(cross, "prow", 4, 1)
            special = [line, cross, line_other, cross_other]
            held = pivots
        elif split:
            special = special + [swap(special[0], "prow", 4, 1)]
        mix, base = call(
            functools.partial(chain_kernel, n_piece, split, len(special)),
            where2,
            [bf(row_dev, columns), bf(row_dev, columns)],
            0,
            held, rows, other, came, rest, put, start_rows, inverses, *special,
            scratch=[pltpu.VMEM((row_dev, columns), BF)] * 2,
        )
        return pl.pallas_call(
            functools.partial(update_kernel, n_piece),
            out_shape=bf(row_dev, columns),
            grid=(row_dev // W,),
            in_specs=[
                pl.BlockSpec((W, columns), lambda i: (i, 0)),
                pl.BlockSpec((8, W), lambda i: (0, i)),
                pl.BlockSpec((row_dev, columns), lambda i: (0, 0)),
            ]
            + [pl.BlockSpec((len(STEPS), W // n_piece, W), lambda i: (0, 0, i))] * n_piece,
            out_specs=pl.BlockSpec((W, columns), lambda i: (i, 0)),
            cost_estimate=COST,
            compiler_params=pltpu.CompilerParams(vmem_limit_bytes=40 * 1024 * 1024),
        )(base, weight, mix, *bulk)

    return on_device


def solution(mesh):
    return jax.shard_map(
        make(mesh.shape["prow"], mesh.shape["pcol"]),
        mesh=mesh,
        in_specs=(P("prow", "pcol"), P(None, "pcol", "prow"), P(None, "prow"), P(), P()),
        out_specs=P("prow", "pcol"),
        check_vma=False,
    )
```

```python
import functools

import jax
import jax.numpy as jnp
from jax import lax
from jax.experimental import pallas as pl
from jax.experimental.pallas import tpu as pltpu
from jax.sharding import PartitionSpec as P

STEPS = (0, 1, 2, 3)
PAIRS = [(k, e) for k in STEPS for e in STEPS if e < k]
BF = jnp.bfloat16
F32 = jnp.float32
I32 = jnp.int32
W = 256
VMEM = pl.BlockSpec(memory_space=pltpu.VMEM)
SMEM = pl.BlockSpec(memory_space=pltpu.SMEM)
COST = pl.CostEstimate(flops=1000, bytes_accessed=1000, transcendentals=0)
FIRST, LOW, HIGH, IS_LOW, ROW, CORE, ME = range(7)


def swap(value, axis, size, mask):
    return lax.ppermute(value, axis, [(i, i ^ mask) for i in range(size)])


def dot_tn(a, b):
    return lax.dot_general(a, b, (((0,), (0,)), ((), ())), preferred_element_type=F32)


def dot_nt(a, b):
    return lax.dot_general(a, b, (((1,), (1,)), ((), ())), preferred_element_type=F32)


def dot(a, b):
    return jnp.dot(a, b, preferred_element_type=F32)


def pivot_views(piv_ref):
    rows = piv_ref[...]
    both = jnp.concatenate([rows, rows], axis=0)
    columns = jnp.transpose(both)
    return (lambda k: rows[k : k + 1, :]), (lambda k: columns[:, k : k + 1])


def matches(steps, row_of, col_of):
    out = {}
    for k in steps:
        found = jnp.zeros((W, 1), I32)
        terms = []
        for e in reversed([e for e in steps if e < k]):
            same = (col_of(k) == row_of(e)).astype(I32)
            same = same * (1 - found)
            terms.append((e, same.astype(F32).astype(BF)))
            found = found + jnp.sum(same, axis=1, keepdims=True)
        out[k] = (terms, found)
    return out


def later_matches(k, e, steps, row_of, col_of):
    found = jnp.zeros((1, W), I32)
    for q in steps:
        if e < q < k:
            found = jnp.maximum(found, jnp.max((col_of(q) == row_of(k)).astype(I32), axis=0, keepdims=True))
    return found


def scale_row(exp_ref, step, lo, count, tile):
    parts = []
    for t in range(lo // tile, (lo + count) // tile):
        e = exp_ref[step, t]
        scale = jnp.where(e >= 0, jnp.where(e == 1, 2.0, 1.0), jnp.where(e == -1, 0.5, jnp.where(e == -2, 0.25, 0.125)))
        parts.append(jnp.full((1, tile), scale, F32))
    return jnp.concatenate(parts, axis=1) if len(parts) > 1 else parts[0]


def pick_rows(scal, col, source, row_dev):
    lane = lax.broadcasted_iota(I32, (W, row_dev), 1) + scal[FIRST]
    sel = (col == lane).astype(F32).astype(BF)
    return dot(sel, source)


def slice_pick_kernel(tile, scal, fac, piv, pan, sp_ref):
    row_dev = pan.shape[2]
    _, col_of = pivot_views(piv)
    is_top = scal[ROW] == 0
    lane = lax.broadcasted_iota(I32, (W, row_dev), 1) + scal[FIRST]
    for k in STEPS[1:]:
        sel = (col_of(k) == lane).astype(F32).astype(BF)
        scaled = jnp.concatenate([pan[e].astype(F32) * scale_row(fac, e, 0, row_dev, tile) for e in STEPS[:k]], axis=0).astype(BF)
        got = dot_nt(scaled, sel)
        top = scaled[:, k * W : (k + 1) * W].astype(F32)
        value = jnp.where(is_top, top, got).astype(BF)
        part = pan.shape[1]
        for e in STEPS[:k]:
            at = PAIRS.index((k, e))
            sp_ref[:, at * W : (at + 1) * W] = value[e * part : (e + 1) * part]


def row_pick_kernel(scal, piv, mat, v_ref):
    _, col_of = pivot_views(piv)
    is_top = scal[ROW] == 0
    for k in STEPS:
        @pl.when(is_top)
        def _():
            v_ref[k * W : (k + 1) * W, :] = mat[k * W : (k + 1) * W, :]

        @pl.when(jnp.logical_not(is_top))
        def _():
            v_ref[k * W : (k + 1) * W, :] = pick_rows(scal, col_of(k), mat[...], mat.shape[0]).astype(BF)


def pass_first(kernel, first, scal, *refs):
    kernel(first, scal, *refs)


def slices_resolved(scal, piv, tops, picks):
    row_of, col_of = pivot_views(piv)
    out = []
    table = matches(STEPS, row_of, col_of)
    for k, e in PAIRS:
        value = picks[(k, e)]
        between = [(q, m) for q, m in table[k][0] if q > e]
        if between:
            moved = sum(dot_nt(tops[(q, e)].astype(BF), m) for q, m in between)
            p = row_of(k)
            here = (p >= scal[LOW]) & (p < scal[HIGH])
            resolve = (later_matches(k, e, STEPS, row_of, col_of) > 0) & (here | (scal[IS_LOW] == 1))
            value = jnp.where(resolve, moved, value)
        out.append(value)
    return out


def here_lanes(scal, piv, k):
    p = piv[k : k + 1, :]
    return (p >= scal[LOW]) & (p < scal[HIGH])


def slice_message_kernel(scal, piv, own, other, out):
    is_top = scal[ROW] == 0
    low = scal[IS_LOW] == 1
    tops, picks, sums = {}, {}, {}
    for at, pair in enumerate(PAIRS):
        lanes = slice(at * W, (at + 1) * W)
        a, b = own[:, lanes].astype(F32), other[:, lanes].astype(F32)
        tops[pair] = jnp.where(is_top, a, b)
        picks[pair] = jnp.where(is_top, b, a)
        sums[pair] = a + b
    resolved = slices_resolved(scal, piv, tops, picks)
    for at, pair in enumerate(PAIRS):
        from_low = jnp.where(here_lanes(scal, piv, pair[0]), resolved[at], tops[pair])
        out[:, at * W : (at + 1) * W] = jnp.where(low, from_low, sums[pair]).astype(BF)


def slice_final_kernel(split, scal, piv, own, other, came, out):
    is_top = scal[ROW] == 0
    low = scal[IS_LOW] == 1
    tops, picks = {}, {}
    for at, pair in enumerate(PAIRS):
        lanes = slice(at * W, (at + 1) * W)
        a, b, c = own[:, lanes].astype(F32), other[:, lanes].astype(F32), came[:, lanes].astype(F32)
        tops[pair] = jnp.where(low, jnp.where(is_top, a, b), c)
        chip = jnp.where(low, jnp.where(is_top, b, a), a + b)
        picks[pair] = jnp.where(here_lanes(scal, piv, pair[0]), chip, c)
    resolved = slices_resolved(scal, piv, tops, picks)
    width = len(PAIRS) * W
    for at, pair in enumerate(PAIRS):
        if split:
            value = jnp.where(scal[CORE] == 0, tops[pair], resolved[at])
            out[:, at * W : (at + 1) * W] = value.astype(BF)
        else:
            out[:, at * W : (at + 1) * W] = tops[pair].astype(BF)
            out[:, width + at * W : width + (at + 1) * W] = resolved[at].astype(BF)


def rows_resolved(scal, steps, table, col_of, tops, picks):
    out = []
    for at, k in enumerate(steps):
        value = picks[at]
        terms, found = table[k]
        if terms:
            moved = sum(dot(m, tops[steps.index(e)].astype(BF)) for e, m in terms)
            p = col_of(k)
            here = (p >= scal[LOW]) & (p < scal[HIGH])
            value = jnp.where((found > 0) & (here | (scal[IS_LOW] == 1)), moved, value)
        out.append(value)
    return out


def here_column(scal, p):
    return (p >= scal[LOW]) & (p < scal[HIGH])


def row_message_kernel(scal, piv, own, other, out):
    steps = STEPS
    row_of, col_of = pivot_views(piv)
    n = len(steps)
    is_top = scal[ROW] == 0
    low = scal[IS_LOW] == 1
    a = [own[i * W : (i + 1) * W, :].astype(F32) for i in range(n)]
    b = [other[i * W : (i + 1) * W, :].astype(F32) for i in range(n)]
    tops = [jnp.where(is_top, x, y) for x, y in zip(a, b)]
    picks = [jnp.where(is_top, y, x) for x, y in zip(a, b)]
    table = matches(steps, row_of, col_of)
    resolved = rows_resolved(scal, steps, table, col_of, tops, picks)
    half = W // 2
    for i, k in enumerate(steps):
        from_low = jnp.where(here_column(scal, col_of(k)), resolved[i], tops[i])
        value = jnp.where(low, from_low, a[i] + b[i])
        out[i * half : (i + 1) * half, :] = jnp.where(scal[CORE] == 0, value[:half], value[half:]).astype(BF)


def prepare_kernel(tile, scal, exps, piv, cur, put_ref, base_ref, weight_ref):
    row_of, col_of = pivot_views(piv)
    row_dev, columns = cur.shape
    top_block = scal[FIRST] == 0
    for lo in range(0, row_dev, W):
        ids = lax.broadcasted_iota(I32, (W, W), 0) + scal[FIRST] + lo
        lane = lax.broadcasted_iota(I32, (W, W), 1) + scal[FIRST] + lo
        taken = jnp.zeros((W, 1), I32)
        alive = jnp.where(top_block, jnp.zeros((1, W), F32), jnp.ones((1, W), F32))
        for k in reversed(STEPS):
            same = (ids == row_of(k)).astype(I32) * (1 - taken)
            put_ref[lo : lo + W, k * W : (k + 1) * W] = same.astype(F32).astype(BF)
            taken = taken + jnp.sum(same, axis=1, keepdims=True)
            weight_ref[k : k + 1, lo : lo + W] = scale_row(exps, k, lo, W, tile) * alive
            if k:
                hit = jnp.max((col_of(k) == lane).astype(F32), axis=0, keepdims=True)
                alive = alive * (1.0 - hit)
        base_ref[lo : lo + W, :] = jnp.where(taken > 0, 0.0, cur[lo : lo + W, :].astype(F32)).astype(BF)


def assemble_kernel(scal, piv, own, other, came, rest, top_ref, pick_ref):
    row_of, col_of = pivot_views(piv)
    is_top = scal[ROW] == 0
    low = scal[IS_LOW] == 1
    core0 = scal[CORE] == 0
    half = W // 2
    tops, picks = [], []
    for k in STEPS:
        a = own[k * W : (k + 1) * W, :].astype(F32)
        b = other[k * W : (k + 1) * W, :].astype(F32)
        c = came[k * half : (k + 1) * half, :].astype(F32)
        d = rest[k * half : (k + 1) * half, :].astype(F32)
        got = jnp.concatenate([jnp.where(core0, c, d), jnp.where(core0, d, c)], axis=0)
        tops.append(jnp.where(low, jnp.where(is_top, a, b), got))
        chip = jnp.where(low, jnp.where(is_top, b, a), a + b)
        picks.append(jnp.where(here_column(scal, col_of(k)), chip, got))
    table = matches(STEPS, row_of, col_of)
    chosen = rows_resolved(scal, STEPS, table, col_of, tops, picks)
    for k in STEPS:
        top_ref[k * W : (k + 1) * W, :] = tops[k].astype(BF)
        pick_ref[k * W : (k + 1) * W, :] = chosen[k].astype(BF)


def chain_kernel(n_piece, split, n_side, scal, *refs):
    _, tops, chosen, put, start_rows, inv = refs[:6]
    sides = refs[6 : 6 + n_side]
    refs = refs[6 + n_side :]
    mix_ref, base_ref, s_ref, u_ref = refs
    row_dev, columns = start_rows.shape
    part = W // n_piece
    top_block = scal[FIRST] == 0
    core0 = scal[CORE] == 0
    def panel_rows(arrays, base):
        if len(arrays) == 1:
            return arrays[0][:, base : base + W]
        line, cross = arrays
        blocks = []
        for z in range(n_piece // 2):
            blocks += [line[z * part : (z + 1) * part, base : base + W], cross[z * part : (z + 1) * part, base : base + W]]
        return jnp.concatenate(blocks, axis=0)

    def side_rows(pair, which):
        base = PAIRS.index(pair) * W
        if not split:
            return panel_rows(sides, base + which * len(PAIRS) * W)
        mine = panel_rows(sides[: n_side // 2], base)
        theirs = panel_rows(sides[n_side // 2 :], base)
        mine_is = core0 if which == 0 else jnp.logical_not(core0)
        return jnp.where(mine_is, mine.astype(F32), theirs.astype(F32)).astype(BF)

    for k in STEPS:
        rows = slice(k * W, (k + 1) * W)
        acc, upper = chosen[rows, :].astype(F32), tops[rows, :].astype(F32)
        for e in STEPS[:k]:
            mixed = mix_ref[e * W : (e + 1) * W, :]
            acc = acc - dot_tn(side_rows((k, e), 1), mixed)
            upper = upper - dot_tn(side_rows((k, e), 0), mixed)
        u_ref[k * W : (k + 1) * W, :] = upper.astype(BF)
        s_ref[k * W : (k + 1) * W, :] = dot(inv[k], acc.astype(BF)).astype(BF)
        for m in range(n_piece):
            if n_piece == 1:
                mix_ref[k * W : (k + 1) * W, :] = s_ref[k * W : (k + 1) * W, :]
                break
            start = pl.multiple_of((scal[ME] ^ m) * part, part)
            mix_ref[k * W + m * part : k * W + (m + 1) * part, :] = s_ref[pl.ds(k * W + start, part), :]

    @pl.when(top_block)
    def _():
        base_ref[...] = s_ref[...]

    @pl.when(jnp.logical_not(top_block))
    def _():
        for lo in range(0, row_dev, W):
            placed = dot(put[lo : lo + W, :], u_ref[...])
            base_ref[lo : lo + W, :] = (start_rows[lo : lo + W, :].astype(F32) + placed).astype(BF)


def update_kernel(n_piece, base, weight, mix, *refs):
    pieces, out = refs[:n_piece], refs[n_piece]
    acc = base[...].astype(F32)
    for k in STEPS:
        block = jnp.concatenate([p[k] for p in pieces], axis=0) * weight[k : k + 1, :].astype(BF)
        acc = acc - dot_tn(block, mix[k * W : (k + 1) * W, :])
    out[...] = acc.astype(BF)


def place(split, row_dev, n_row, summed):
    row = lax.axis_index("prow")
    me = lax.axis_index("pcol")
    first = row * row_dev
    if split:
        chip = row // 2
        return [first, chip * 2 * row_dev, (chip + 1) * 2 * row_dev, (chip == 0).astype(I32), row, row % 2, me]
    return [first, 0, n_row * row_dev, 1, 1 if summed else row, 0, me]


def call(kernel, where, shapes, n_smem, *args, scratch=()):
    single = not isinstance(shapes, (list, tuple))

    def body(*refs):
        kernel(place(*where), *refs)

    return pl.pallas_call(
        body,
        out_shape=shapes,
        in_specs=[SMEM] * n_smem + [VMEM] * (len(args) - n_smem),
        out_specs=VMEM if single else [VMEM] * len(shapes),
        scratch_shapes=list(scratch),
        cost_estimate=COST,
        compiler_params=pltpu.CompilerParams(vmem_limit_bytes=40 * 1024 * 1024),
    )(*args)


def gather(own, axis):
    return [lax.all_gather(own, "pcol", axis=axis, tiled=True)]


def after(value, *others):
    return lax.optimization_barrier((value,) + others)[0]


def make(n_row, n_col):
    split = n_row == 4 and n_col == 8
    n_piece = 8 if split else 1

    def psum_pair(own, row):
        zero = jnp.zeros_like(own)
        picks = lax.psum(jnp.where(row == 0, zero, own), "prow")
        tops = lax.psum(jnp.where(row == 0, own, zero), "prow")
        return picks.astype(F32).astype(BF), tops.astype(F32).astype(BF)

    def on_device(matrix, panels, exponents, inverses, pivots):
        row_dev, columns = matrix.shape
        assert len(STEPS) * W == row_dev and pivots.shape == (len(STEPS), W)
        tile = row_dev // exponents.shape[1]
        part = W // n_col
        row = lax.axis_index("prow")
        where = (split, row_dev, n_row, False)
        where2 = (split, row_dev, n_row, True)
        wide = len(PAIRS) * W
        bf = lambda *shape: jax.ShapeDtypeStruct(shape, BF)

        sp = call(functools.partial(pass_first, slice_pick_kernel, tile), where, bf(part, wide), 1, exponents, pivots, panels)
        rows = call(row_pick_kernel, where, bf(row_dev, columns), 0, pivots, matrix)
        load = wide if split else 2 * wide
        final_slices = functools.partial(pass_first, slice_final_kernel, split)
        if split:
            sp_other = swap(sp, "prow", 4, 1)
            message = call(slice_message_kernel, where, bf(part, wide), 0, pivots, sp, sp_other)
            sp_came = swap(message, "prow", 4, 2)
        else:
            sp, sp_other = psum_pair(sp, row)
            sp_came = sp
        put, start_rows, weight = call(
            functools.partial(pass_first, prepare_kernel, tile),
            where,
            [bf(row_dev, row_dev), bf(row_dev, columns), jax.ShapeDtypeStruct((8, row_dev), F32)],
            1,
            exponents, after(pivots, sp), matrix,
        )
        if n_piece == 8:
            bz2 = swap(panels, "pcol", 8, 4)
            bx0 = swap(panels, "pcol", 8, 1)
            bz1 = swap(panels, "pcol", 8, 2)
            sp_came = after(sp_came, bx0, weight)
            own = call(final_slices, where2, bf(part, load), 0, pivots, sp, sp_other, sp_came)
        else:
            own = call(final_slices, where2, bf(part, load), 0, pivots, sp, sp_other, sp_came)
            bulk, special = gather(panels, 1), gather(own, 0)
        if split:
            other = swap(rows, "prow", 4, 1)
            message = call(row_message_kernel, where, bf(row_dev // 2, columns), 0, after(pivots, own, bz2), rows, other)
            came = swap(message, "prow", 4, 2)
            rest = None
        else:
            message = rows
            rows, other = psum_pair(rows, row)
            came = rest = rows[: row_dev // 2]
        held = pivots
        if n_piece == 8:
            sz2 = swap(after(own, message, bz1), "pcol", 8, 4)
            sz3 = swap(own, "pcol", 8, 6)
            sz1 = swap(own, "pcol", 8, 2)
            bz3 = swap(after(panels, bz2, sz2), "pcol", 8, 6)
            line = jnp.concatenate([own, sz1, sz2, sz3], axis=0)
            cross = swap(line, "pcol", 8, 1)
            bz2x = swap(after(bz2, sz3), "pcol", 8, 1)
            bz3x = swap(bz3, "pcol", 8, 1)
            line_other = swap(line, "prow", 4, 1)
            bz1x = swap(after(bx0, sz1), "pcol", 8, 2)
            rest = swap(after(came, bz2x, bz1x), "prow", 4, 1)
            bulk = [panels, bx0, bz1, bz1x, bz2, bz2x, bz3, bz3x]
            cross_other = swap(after(cross, bz3), "prow", 4, 1)
            special = [line, cross, line_other, cross_other]
            held = pivots
        elif split:
            special = special + [swap(special[0], "prow", 4, 1)]
        tops, chosen = call(assemble_kernel, where2, [bf(row_dev, columns)] * 2, 0, pivots, rows, other, came, rest)
        mix, base = call(
            functools.partial(chain_kernel, n_piece, split, len(special)),
            where2,
            [bf(row_dev, columns), bf(row_dev, columns)],
            0,
            held, tops, chosen, put, start_rows, inverses, *special,
            scratch=[pltpu.VMEM((row_dev, columns), BF)] * 2,
        )
        return pl.pallas_call(
            functools.partial(update_kernel, n_piece),
            out_shape=bf(row_dev, columns),
            grid=(row_dev // W,),
            in_specs=[
                pl.BlockSpec((W, columns), lambda i: (i, 0)),
                pl.BlockSpec((8, W), lambda i: (0, i)),
                pl.BlockSpec((row_dev, columns), lambda i: (0, 0)),
            ]
            + [pl.BlockSpec((len(STEPS), W // n_piece, W), lambda i: (0, 0, i))] * n_piece,
            out_specs=pl.BlockSpec((W, columns), lambda i: (i, 0)),
            cost_estimate=COST,
            compiler_params=pltpu.CompilerParams(vmem_limit_bytes=40 * 1024 * 1024),
        )(base, weight, mix, *bulk)

    return on_device


def solution(mesh):
    return jax.shard_map(
        make(mesh.shape["prow"], mesh.shape["pcol"]),
        mesh=mesh,
        in_specs=(P("prow", "pcol"), P(None, "pcol", "prow"), P(None, "prow"), P(), P()),
        out_specs=P("prow", "pcol"),
        check_vma=False,
    )
```

```python
import functools

import jax
import jax.numpy as jnp
from jax import lax
from jax.experimental import pallas as pl
from jax.experimental.pallas import tpu as pltpu
from jax.sharding import PartitionSpec as P

STEPS = (0, 1, 2, 3)
PAIRS = [(k, e) for k in STEPS for e in STEPS if e < k]
BF = jnp.bfloat16
F32 = jnp.float32
I32 = jnp.int32
W = 256
VMEM = pl.BlockSpec(memory_space=pltpu.VMEM)
SMEM = pl.BlockSpec(memory_space=pltpu.SMEM)
COST = pl.CostEstimate(flops=1000, bytes_accessed=1000, transcendentals=0)
FIRST, LOW, HIGH, IS_LOW, ROW, CORE, ME = range(7)


def swap(value, axis, size, mask):
    return lax.ppermute(value, axis, [(i, i ^ mask) for i in range(size)])


def dot_tn(a, b):
    return lax.dot_general(a, b, (((0,), (0,)), ((), ())), preferred_element_type=F32)


def dot_nt(a, b):
    return lax.dot_general(a, b, (((1,), (1,)), ((), ())), preferred_element_type=F32)


def dot(a, b):
    return jnp.dot(a, b, preferred_element_type=F32)


def pivot_views(piv_ref):
    rows = piv_ref[...]
    both = jnp.concatenate([rows, rows], axis=0)
    columns = jnp.transpose(both)
    return (lambda k: rows[k : k + 1, :]), (lambda k: columns[:, k : k + 1])


def matches(steps, row_of, col_of):
    out = {}
    for k in steps:
        found = jnp.zeros((W, 1), I32)
        terms = []
        for e in reversed([e for e in steps if e < k]):
            same = (col_of(k) == row_of(e)).astype(I32)
            same = same * (1 - found)
            terms.append((e, same.astype(F32).astype(BF)))
            found = found + jnp.sum(same, axis=1, keepdims=True)
        out[k] = (terms, found)
    return out


def later_matches(k, e, steps, row_of, col_of):
    found = jnp.zeros((1, W), I32)
    for q in steps:
        if e < q < k:
            found = jnp.maximum(found, jnp.max((col_of(q) == row_of(k)).astype(I32), axis=0, keepdims=True))
    return found


def scale_row(exp_ref, step, lo, count, tile):
    parts = []
    for t in range(lo // tile, (lo + count) // tile):
        e = exp_ref[step, t]
        scale = jnp.where(e >= 0, jnp.where(e == 1, 2.0, 1.0), jnp.where(e == -1, 0.5, jnp.where(e == -2, 0.25, 0.125)))
        parts.append(jnp.full((1, tile), scale, F32))
    return jnp.concatenate(parts, axis=1) if len(parts) > 1 else parts[0]


def pick_rows(scal, col, source, row_dev):
    lane = lax.broadcasted_iota(I32, (W, row_dev), 1) + scal[FIRST]
    sel = (col == lane).astype(F32).astype(BF)
    return dot(sel, source)


def slice_pick_kernel(tile, scal, fac, piv, pan, sp_ref):
    row_dev = pan.shape[2]
    _, col_of = pivot_views(piv)
    is_top = scal[ROW] == 0
    lane = lax.broadcasted_iota(I32, (W, row_dev), 1) + scal[FIRST]
    for k in STEPS[1:]:
        sel = (col_of(k) == lane).astype(F32).astype(BF)
        scaled = jnp.concatenate([pan[e].astype(F32) * scale_row(fac, e, 0, row_dev, tile) for e in STEPS[:k]], axis=0).astype(BF)
        got = dot_nt(scaled, sel)
        top = scaled[:, k * W : (k + 1) * W].astype(F32)
        value = jnp.where(is_top, top, got).astype(BF)
        part = pan.shape[1]
        for e in STEPS[:k]:
            at = PAIRS.index((k, e))
            sp_ref[:, at * W : (at + 1) * W] = value[e * part : (e + 1) * part]


def row_pick_kernel(scal, piv, mat, v_ref):
    _, col_of = pivot_views(piv)
    is_top = scal[ROW] == 0
    for k in STEPS:
        @pl.when(is_top)
        def _():
            v_ref[k * W : (k + 1) * W, :] = mat[k * W : (k + 1) * W, :]

        @pl.when(jnp.logical_not(is_top))
        def _():
            v_ref[k * W : (k + 1) * W, :] = pick_rows(scal, col_of(k), mat[...], mat.shape[0]).astype(BF)


def pass_first(kernel, first, scal, *refs):
    kernel(first, scal, *refs)


def slices_resolved(scal, piv, tops, picks):
    row_of, col_of = pivot_views(piv)
    out = []
    table = matches(STEPS, row_of, col_of)
    for k, e in PAIRS:
        value = picks[(k, e)]
        between = [(q, m) for q, m in table[k][0] if q > e]
        if between:
            moved = sum(dot_nt(tops[(q, e)].astype(BF), m) for q, m in between)
            p = row_of(k)
            here = (p >= scal[LOW]) & (p < scal[HIGH])
            resolve = (later_matches(k, e, STEPS, row_of, col_of) > 0) & (here | (scal[IS_LOW] == 1))
            value = jnp.where(resolve, moved, value)
        out.append(value)
    return out


def here_lanes(scal, piv, k):
    p = piv[k : k + 1, :]
    return (p >= scal[LOW]) & (p < scal[HIGH])


def slice_message_kernel(scal, piv, own, other, out):
    is_top = scal[ROW] == 0
    low = scal[IS_LOW] == 1
    tops, picks, sums = {}, {}, {}
    for at, pair in enumerate(PAIRS):
        lanes = slice(at * W, (at + 1) * W)
        a, b = own[:, lanes].astype(F32), other[:, lanes].astype(F32)
        tops[pair] = jnp.where(is_top, a, b)
        picks[pair] = jnp.where(is_top, b, a)
        sums[pair] = a + b
    resolved = slices_resolved(scal, piv, tops, picks)
    for at, pair in enumerate(PAIRS):
        from_low = jnp.where(here_lanes(scal, piv, pair[0]), resolved[at], tops[pair])
        out[:, at * W : (at + 1) * W] = jnp.where(low, from_low, sums[pair]).astype(BF)


def slice_final_kernel(split, scal, piv, own, other, came, out):
    is_top = scal[ROW] == 0
    low = scal[IS_LOW] == 1
    tops, picks = {}, {}
    for at, pair in enumerate(PAIRS):
        lanes = slice(at * W, (at + 1) * W)
        a, b, c = own[:, lanes].astype(F32), other[:, lanes].astype(F32), came[:, lanes].astype(F32)
        tops[pair] = jnp.where(low, jnp.where(is_top, a, b), c)
        chip = jnp.where(low, jnp.where(is_top, b, a), a + b)
        picks[pair] = jnp.where(here_lanes(scal, piv, pair[0]), chip, c)
    resolved = slices_resolved(scal, piv, tops, picks)
    width = len(PAIRS) * W
    for at, pair in enumerate(PAIRS):
        if split:
            value = jnp.where(scal[CORE] == 0, tops[pair], resolved[at])
            out[:, at * W : (at + 1) * W] = value.astype(BF)
        else:
            out[:, at * W : (at + 1) * W] = tops[pair].astype(BF)
            out[:, width + at * W : width + (at + 1) * W] = resolved[at].astype(BF)


def rows_resolved(scal, steps, table, col_of, tops, picks):
    out = []
    for at, k in enumerate(steps):
        value = picks[at]
        terms, found = table[k]
        if terms:
            moved = sum(dot(m, tops[steps.index(e)].astype(BF)) for e, m in terms)
            p = col_of(k)
            here = (p >= scal[LOW]) & (p < scal[HIGH])
            value = jnp.where((found > 0) & (here | (scal[IS_LOW] == 1)), moved, value)
        out.append(value)
    return out


def here_column(scal, p):
    return (p >= scal[LOW]) & (p < scal[HIGH])


def row_message_kernel(scal, piv, own, other, out):
    steps = STEPS
    row_of, col_of = pivot_views(piv)
    n = len(steps)
    is_top = scal[ROW] == 0
    low = scal[IS_LOW] == 1
    a = [own[i * W : (i + 1) * W, :].astype(F32) for i in range(n)]
    b = [other[i * W : (i + 1) * W, :].astype(F32) for i in range(n)]
    tops = [jnp.where(is_top, x, y) for x, y in zip(a, b)]
    picks = [jnp.where(is_top, y, x) for x, y in zip(a, b)]
    table = matches(steps, row_of, col_of)
    resolved = rows_resolved(scal, steps, table, col_of, tops, picks)
    half = W // 2
    for i, k in enumerate(steps):
        from_low = jnp.where(here_column(scal, col_of(k)), resolved[i], tops[i])
        value = jnp.where(low, from_low, a[i] + b[i])
        out[i * half : (i + 1) * half, :] = jnp.where(scal[CORE] == 0, value[:half], value[half:]).astype(BF)


def prepare_kernel(tile, scal, exps, piv, cur, put_ref, base_ref, weight_ref):
    row_of, col_of = pivot_views(piv)
    row_dev, columns = cur.shape
    top_block = scal[FIRST] == 0
    for lo in range(0, row_dev, W):
        ids = lax.broadcasted_iota(I32, (W, W), 0) + scal[FIRST] + lo
        lane = lax.broadcasted_iota(I32, (W, W), 1) + scal[FIRST] + lo
        taken = jnp.zeros((W, 1), I32)
        alive = jnp.where(top_block, jnp.zeros((1, W), F32), jnp.ones((1, W), F32))
        for k in reversed(STEPS):
            same = (ids == row_of(k)).astype(I32) * (1 - taken)
            put_ref[lo : lo + W, k * W : (k + 1) * W] = same.astype(F32).astype(BF)
            taken = taken + jnp.sum(same, axis=1, keepdims=True)
            weight_ref[k : k + 1, lo : lo + W] = scale_row(exps, k, lo, W, tile) * alive
            if k:
                hit = jnp.max((col_of(k) == lane).astype(F32), axis=0, keepdims=True)
                alive = alive * (1.0 - hit)
        base_ref[lo : lo + W, :] = jnp.where(taken > 0, 0.0, cur[lo : lo + W, :].astype(F32)).astype(BF)


def assemble_kernel(scal, piv, own, other, came, rest, top_ref, pick_ref):
    row_of, col_of = pivot_views(piv)
    is_top = scal[ROW] == 0
    low = scal[IS_LOW] == 1
    core0 = scal[CORE] == 0
    half = W // 2
    tops, picks = [], []
    for k in STEPS:
        a = own[k * W : (k + 1) * W, :].astype(F32)
        b = other[k * W : (k + 1) * W, :].astype(F32)
        c = came[k * half : (k + 1) * half, :].astype(F32)
        d = rest[k * half : (k + 1) * half, :].astype(F32)
        got = jnp.concatenate([jnp.where(core0, c, d), jnp.where(core0, d, c)], axis=0)
        tops.append(jnp.where(low, jnp.where(is_top, a, b), got))
        chip = jnp.where(low, jnp.where(is_top, b, a), a + b)
        picks.append(jnp.where(here_column(scal, col_of(k)), chip, got))
    table = matches(STEPS, row_of, col_of)
    chosen = rows_resolved(scal, STEPS, table, col_of, tops, picks)
    for k in STEPS:
        top_ref[k * W : (k + 1) * W, :] = tops[k].astype(BF)
        pick_ref[k * W : (k + 1) * W, :] = chosen[k].astype(BF)


def chain_kernel(n_piece, split, n_side, scal, *refs):
    _, tops, chosen, put, start_rows, inv = refs[:6]
    sides = refs[6 : 6 + n_side]
    refs = refs[6 + n_side :]
    weight, pieces = refs[0], refs[1:n_piece]
    mix_ref, base_ref, s_ref, u_ref = refs[n_piece:]
    row_dev, columns = start_rows.shape
    part = W // n_piece
    top_block = scal[FIRST] == 0
    core0 = scal[CORE] == 0
    def panel_rows(arrays, base):
        if len(arrays) == 1:
            return arrays[0][:, base : base + W]
        line, cross = arrays
        blocks = []
        for z in range(n_piece // 2):
            blocks += [line[z * part : (z + 1) * part, base : base + W], cross[z * part : (z + 1) * part, base : base + W]]
        return jnp.concatenate(blocks, axis=0)

    def side_rows(pair, which):
        base = PAIRS.index(pair) * W
        if not split:
            return panel_rows(sides, base + which * len(PAIRS) * W)
        mine = panel_rows(sides[: n_side // 2], base)
        theirs = panel_rows(sides[n_side // 2 :], base)
        mine_is = core0 if which == 0 else jnp.logical_not(core0)
        return jnp.where(mine_is, mine.astype(F32), theirs.astype(F32)).astype(BF)

    for k in STEPS:
        rows = slice(k * W, (k + 1) * W)
        acc, upper = chosen[rows, :].astype(F32), tops[rows, :].astype(F32)
        for e in STEPS[:k]:
            mixed = mix_ref[e * W : (e + 1) * W, :]
            acc = acc - dot_tn(side_rows((k, e), 1), mixed)
            upper = upper - dot_tn(side_rows((k, e), 0), mixed)
        u_ref[k * W : (k + 1) * W, :] = upper.astype(BF)
        s_ref[k * W : (k + 1) * W, :] = dot(inv[k], acc.astype(BF)).astype(BF)
        for m in range(n_piece):
            if n_piece == 1:
                mix_ref[k * W : (k + 1) * W, :] = s_ref[k * W : (k + 1) * W, :]
                break
            start = pl.multiple_of((scal[ME] ^ m) * part, part)
            mix_ref[k * W + m * part : k * W + (m + 1) * part, :] = s_ref[pl.ds(k * W + start, part), :]

    @pl.when(top_block)
    def _():
        base_ref[...] = s_ref[...].astype(F32)

    @pl.when(jnp.logical_not(top_block))
    def _():
        early = (n_piece - 1) * part
        for lo in range(0, row_dev, W):
            rows = slice(lo, lo + W)
            acc = start_rows[rows, :].astype(F32) + dot(put[rows, :], u_ref[...])
            for k in STEPS:
                if early:
                    block = jnp.concatenate([p[k, :, rows] for p in pieces], axis=0) * weight[k : k + 1, rows].astype(BF)
                    acc = acc - dot_tn(block, mix_ref[k * W : k * W + early, :])
            base_ref[rows, :] = acc


def update_kernel(base, weight, mix, last, out):
    rows = pl.ds(pl.multiple_of(pl.program_id(0) * out.shape[0], out.shape[0]), out.shape[0])
    part = last.shape[1]
    block = jnp.concatenate([last[k, :, rows] * weight[k : k + 1, rows].astype(BF) for k in STEPS], axis=0)
    mixed = jnp.concatenate([mix[(k + 1) * W - part : (k + 1) * W, :] for k in STEPS], axis=0)
    out[...] = (base[...] - dot_tn(block, mixed)).astype(BF)


def place(split, row_dev, n_row, summed):
    row = lax.axis_index("prow")
    me = lax.axis_index("pcol")
    first = row * row_dev
    if split:
        chip = row // 2
        return [first, chip * 2 * row_dev, (chip + 1) * 2 * row_dev, (chip == 0).astype(I32), row, row % 2, me]
    return [first, 0, n_row * row_dev, 1, 1 if summed else row, 0, me]


def call(kernel, where, shapes, n_smem, *args, scratch=()):
    single = not isinstance(shapes, (list, tuple))

    def body(*refs):
        kernel(place(*where), *refs)

    return pl.pallas_call(
        body,
        out_shape=shapes,
        in_specs=[SMEM] * n_smem + [VMEM] * (len(args) - n_smem),
        out_specs=VMEM if single else [VMEM] * len(shapes),
        scratch_shapes=list(scratch),
        cost_estimate=COST,
        compiler_params=pltpu.CompilerParams(vmem_limit_bytes=40 * 1024 * 1024),
    )(*args)


def gather(own, axis):
    return [lax.all_gather(own, "pcol", axis=axis, tiled=True)]


def after(value, *others):
    return lax.optimization_barrier((value,) + others)[0]


def make(n_row, n_col):
    split = n_row == 4 and n_col == 8
    n_piece = 8 if split else 1

    def psum_pair(own, row):
        zero = jnp.zeros_like(own)
        picks = lax.psum(jnp.where(row == 0, zero, own), "prow")
        tops = lax.psum(jnp.where(row == 0, own, zero), "prow")
        return picks.astype(F32).astype(BF), tops.astype(F32).astype(BF)

    def on_device(matrix, panels, exponents, inverses, pivots):
        row_dev, columns = matrix.shape
        assert len(STEPS) * W == row_dev and pivots.shape == (len(STEPS), W)
        tile = row_dev // exponents.shape[1]
        part = W // n_col
        row = lax.axis_index("prow")
        where = (split, row_dev, n_row, False)
        where2 = (split, row_dev, n_row, True)
        wide = len(PAIRS) * W
        bf = lambda *shape: jax.ShapeDtypeStruct(shape, BF)

        sp = call(functools.partial(pass_first, slice_pick_kernel, tile), where, bf(part, wide), 1, exponents, pivots, panels)
        rows = call(row_pick_kernel, where, bf(row_dev, columns), 0, pivots, matrix)
        load = wide if split else 2 * wide
        final_slices = functools.partial(pass_first, slice_final_kernel, split)
        if split:
            sp_other = swap(sp, "prow", 4, 1)
            message = call(slice_message_kernel, where, bf(part, wide), 0, pivots, sp, sp_other)
            sp_came = swap(message, "prow", 4, 2)
        else:
            sp, sp_other = psum_pair(sp, row)
            sp_came = sp
        put, start_rows, weight = call(
            functools.partial(pass_first, prepare_kernel, tile),
            where,
            [bf(row_dev, row_dev), bf(row_dev, columns), jax.ShapeDtypeStruct((8, row_dev), F32)],
            1,
            exponents, after(pivots, sp), matrix,
        )
        if n_piece == 8:
            bz2 = swap(panels, "pcol", 8, 4)
            bx0 = swap(panels, "pcol", 8, 1)
            bz1 = swap(panels, "pcol", 8, 2)
            sp_came = after(sp_came, bx0, weight)
            own = call(final_slices, where2, bf(part, load), 0, pivots, sp, sp_other, sp_came)
        else:
            own = call(final_slices, where2, bf(part, load), 0, pivots, sp, sp_other, sp_came)
            bulk, special = gather(panels, 1), gather(own, 0)
        if split:
            other = swap(rows, "prow", 4, 1)
            message = call(row_message_kernel, where, bf(row_dev // 2, columns), 0, after(pivots, own, bz2), rows, other)
            came = swap(message, "prow", 4, 2)
            rest = None
        else:
            message = rows
            rows, other = psum_pair(rows, row)
            came = rest = rows[: row_dev // 2]
        held = pivots
        if n_piece == 8:
            sz2 = swap(after(own, message, bz1), "pcol", 8, 4)
            sz3 = swap(own, "pcol", 8, 6)
            sz1 = swap(own, "pcol", 8, 2)
            bz3 = swap(after(panels, bz2, sz2), "pcol", 8, 6)
            line = jnp.concatenate([own, sz1, sz2, sz3], axis=0)
            cross = swap(line, "pcol", 8, 1)
            bz2x = swap(after(bz2, sz3), "pcol", 8, 1)
            bz3x = swap(bz3, "pcol", 8, 1)
            line_other = swap(line, "prow", 4, 1)
            bz1x = swap(after(bx0, sz1), "pcol", 8, 2)
            rest = swap(after(came, bz2x, bz1x), "prow", 4, 1)
            bulk = [panels, bx0, bz1, bz1x, bz2, bz2x, bz3, bz3x]
            cross_other = swap(after(cross, bz3), "prow", 4, 1)
            special = [line, cross, line_other, cross_other]
            held = pivots
        elif split:
            special = special + [swap(special[0], "prow", 4, 1)]
        tops, chosen = call(assemble_kernel, where2, [bf(row_dev, columns)] * 2, 0, pivots, rows, other, came, rest)
        mix, base = call(
            functools.partial(chain_kernel, n_piece, split, len(special)),
            where2,
            [bf(row_dev, columns), jax.ShapeDtypeStruct((row_dev, columns), F32)],
            0,
            held, tops, chosen, put, start_rows, inverses, *special, weight, *bulk[:-1],
            scratch=[pltpu.VMEM((row_dev, columns), BF)] * 2,
        )
        return pl.pallas_call(
            update_kernel,
            out_shape=bf(row_dev, columns),
            grid=(row_dev // 512,),
            in_specs=[pl.BlockSpec((512, columns), lambda i: (i, 0))] + [VMEM] * 3,
            out_specs=pl.BlockSpec((512, columns), lambda i: (i, 0)),
            cost_estimate=COST,
            compiler_params=pltpu.CompilerParams(vmem_limit_bytes=40 * 1024 * 1024),
        )(base, weight, mix, bulk[-1])

    return on_device


def solution(mesh):
    return jax.shard_map(
        make(mesh.shape["prow"], mesh.shape["pcol"]),
        mesh=mesh,
        in_specs=(P("prow", "pcol"), P(None, "pcol", "prow"), P(None, "prow"), P(), P()),
        out_specs=P("prow", "pcol"),
        check_vma=False,
    )
```

```python
import functools

import jax
import jax.numpy as jnp
from jax import lax
from jax.experimental import pallas as pl
from jax.experimental.pallas import tpu as pltpu
from jax.sharding import PartitionSpec as P

STEPS = (0, 1, 2, 3)
PAIRS = [(k, e) for k in STEPS for e in STEPS if e < k]
BF = jnp.bfloat16
F32 = jnp.float32
I32 = jnp.int32
W = 256
VMEM = pl.BlockSpec(memory_space=pltpu.VMEM)
SMEM = pl.BlockSpec(memory_space=pltpu.SMEM)
COST = pl.CostEstimate(flops=1000, bytes_accessed=1000, transcendentals=0)
FIRST, LOW, HIGH, IS_LOW, ROW, CORE, ME = range(7)


def swap(value, axis, size, mask):
    return lax.ppermute(value, axis, [(i, i ^ mask) for i in range(size)])


def dot_tn(a, b):
    return lax.dot_general(a, b, (((0,), (0,)), ((), ())), preferred_element_type=F32)


def dot_nt(a, b):
    return lax.dot_general(a, b, (((1,), (1,)), ((), ())), preferred_element_type=F32)


def dot(a, b):
    return jnp.dot(a, b, preferred_element_type=F32)


def pivot_views(piv_ref):
    rows = piv_ref[...]
    both = jnp.concatenate([rows, rows], axis=0)
    columns = jnp.transpose(both)
    return (lambda k: rows[k : k + 1, :]), (lambda k: columns[:, k : k + 1])


def matches(steps, row_of, col_of):
    out = {}
    for k in steps:
        found = jnp.zeros((W, 1), I32)
        terms = []
        for e in reversed([e for e in steps if e < k]):
            same = (col_of(k) == row_of(e)).astype(I32)
            same = same * (1 - found)
            terms.append((e, same.astype(F32).astype(BF)))
            found = found + jnp.sum(same, axis=1, keepdims=True)
        out[k] = (terms, found)
    return out


def later_matches(k, e, steps, row_of, col_of):
    found = jnp.zeros((1, W), I32)
    for q in steps:
        if e < q < k:
            found = jnp.maximum(found, jnp.max((col_of(q) == row_of(k)).astype(I32), axis=0, keepdims=True))
    return found


def scale_row(exp_ref, step, lo, count, tile):
    parts = []
    for t in range(lo // tile, (lo + count) // tile):
        e = exp_ref[step, t]
        scale = jnp.where(e >= 0, jnp.where(e == 1, 2.0, 1.0), jnp.where(e == -1, 0.5, jnp.where(e == -2, 0.25, 0.125)))
        parts.append(jnp.full((1, tile), scale, F32))
    return jnp.concatenate(parts, axis=1) if len(parts) > 1 else parts[0]


def pick_rows(scal, col, source, row_dev):
    lane = lax.broadcasted_iota(I32, (W, row_dev), 1) + scal[FIRST]
    sel = (col == lane).astype(F32).astype(BF)
    return dot(sel, source)


def slice_pick_kernel(tile, scal, fac, piv, pan, sp_ref):
    row_dev = pan.shape[2]
    _, col_of = pivot_views(piv)
    is_top = scal[ROW] == 0
    lane = lax.broadcasted_iota(I32, (W, row_dev), 1) + scal[FIRST]
    for k in STEPS[1:]:
        sel = (col_of(k) == lane).astype(F32).astype(BF)
        scaled = jnp.concatenate([pan[e].astype(F32) * scale_row(fac, e, 0, row_dev, tile) for e in STEPS[:k]], axis=0).astype(BF)
        got = dot_nt(scaled, sel)
        top = scaled[:, k * W : (k + 1) * W].astype(F32)
        value = jnp.where(is_top, top, got).astype(BF)
        part = pan.shape[1]
        for e in STEPS[:k]:
            at = PAIRS.index((k, e))
            sp_ref[:, at * W : (at + 1) * W] = value[e * part : (e + 1) * part]


def row_pick_kernel(scal, piv, mat, v_ref):
    _, col_of = pivot_views(piv)
    is_top = scal[ROW] == 0
    for k in STEPS:
        @pl.when(is_top)
        def _():
            v_ref[k * W : (k + 1) * W, :] = mat[k * W : (k + 1) * W, :]

        @pl.when(jnp.logical_not(is_top))
        def _():
            v_ref[k * W : (k + 1) * W, :] = pick_rows(scal, col_of(k), mat[...], mat.shape[0]).astype(BF)


def pass_first(kernel, first, scal, *refs):
    kernel(first, scal, *refs)


def slices_resolved(scal, piv, tops, picks):
    row_of, col_of = pivot_views(piv)
    out = []
    table = matches(STEPS, row_of, col_of)
    for k, e in PAIRS:
        value = picks[(k, e)]
        between = [(q, m) for q, m in table[k][0] if q > e]
        if between:
            moved = sum(dot_nt(tops[(q, e)].astype(BF), m) for q, m in between)
            p = row_of(k)
            here = (p >= scal[LOW]) & (p < scal[HIGH])
            resolve = (later_matches(k, e, STEPS, row_of, col_of) > 0) & (here | (scal[IS_LOW] == 1))
            value = jnp.where(resolve, moved, value)
        out.append(value)
    return out


def here_lanes(scal, piv, k):
    p = piv[k : k + 1, :]
    return (p >= scal[LOW]) & (p < scal[HIGH])


def slice_message_kernel(scal, piv, own, other, out):
    is_top = scal[ROW] == 0
    low = scal[IS_LOW] == 1
    tops, picks, sums = {}, {}, {}
    for at, pair in enumerate(PAIRS):
        lanes = slice(at * W, (at + 1) * W)
        a, b = own[:, lanes].astype(F32), other[:, lanes].astype(F32)
        tops[pair] = jnp.where(is_top, a, b)
        picks[pair] = jnp.where(is_top, b, a)
        sums[pair] = a + b
    resolved = slices_resolved(scal, piv, tops, picks)
    for at, pair in enumerate(PAIRS):
        from_low = jnp.where(here_lanes(scal, piv, pair[0]), resolved[at], tops[pair])
        out[:, at * W : (at + 1) * W] = jnp.where(low, from_low, sums[pair]).astype(BF)


def slice_final_kernel(split, scal, piv, own, other, came, out):
    is_top = scal[ROW] == 0
    low = scal[IS_LOW] == 1
    tops, picks = {}, {}
    for at, pair in enumerate(PAIRS):
        lanes = slice(at * W, (at + 1) * W)
        a, b, c = own[:, lanes].astype(F32), other[:, lanes].astype(F32), came[:, lanes].astype(F32)
        tops[pair] = jnp.where(low, jnp.where(is_top, a, b), c)
        chip = jnp.where(low, jnp.where(is_top, b, a), a + b)
        picks[pair] = jnp.where(here_lanes(scal, piv, pair[0]), chip, c)
    resolved = slices_resolved(scal, piv, tops, picks)
    width = len(PAIRS) * W
    for at, pair in enumerate(PAIRS):
        if split:
            value = jnp.where(scal[CORE] == 0, tops[pair], resolved[at])
            out[:, at * W : (at + 1) * W] = value.astype(BF)
        else:
            out[:, at * W : (at + 1) * W] = tops[pair].astype(BF)
            out[:, width + at * W : width + (at + 1) * W] = resolved[at].astype(BF)


def rows_resolved(scal, steps, table, col_of, tops, picks):
    out = []
    for at, k in enumerate(steps):
        value = picks[at]
        terms, found = table[k]
        if terms:
            moved = sum(dot(m, tops[steps.index(e)].astype(BF)) for e, m in terms)
            p = col_of(k)
            here = (p >= scal[LOW]) & (p < scal[HIGH])
            value = jnp.where((found > 0) & (here | (scal[IS_LOW] == 1)), moved, value)
        out.append(value)
    return out


def here_column(scal, p):
    return (p >= scal[LOW]) & (p < scal[HIGH])


def row_message_kernel(scal, piv, own, other, out):
    steps = STEPS
    row_of, col_of = pivot_views(piv)
    n = len(steps)
    is_top = scal[ROW] == 0
    low = scal[IS_LOW] == 1
    a = [own[i * W : (i + 1) * W, :].astype(F32) for i in range(n)]
    b = [other[i * W : (i + 1) * W, :].astype(F32) for i in range(n)]
    tops = [jnp.where(is_top, x, y) for x, y in zip(a, b)]
    picks = [jnp.where(is_top, y, x) for x, y in zip(a, b)]
    table = matches(steps, row_of, col_of)
    resolved = rows_resolved(scal, steps, table, col_of, tops, picks)
    half = W // 2
    for i, k in enumerate(steps):
        from_low = jnp.where(here_column(scal, col_of(k)), resolved[i], tops[i])
        value = jnp.where(low, from_low, a[i] + b[i])
        out[i * half : (i + 1) * half, :] = jnp.where(scal[CORE] == 0, value[:half], value[half:]).astype(BF)


def prepare_kernel(tile, scal, exps, piv, cur, put_ref, base_ref, weight_ref):
    row_of, col_of = pivot_views(piv)
    row_dev, columns = cur.shape
    top_block = scal[FIRST] == 0
    for lo in range(0, row_dev, W):
        ids = lax.broadcasted_iota(I32, (W, W), 0) + scal[FIRST] + lo
        lane = lax.broadcasted_iota(I32, (W, W), 1) + scal[FIRST] + lo
        taken = jnp.zeros((W, 1), I32)
        alive = jnp.where(top_block, jnp.zeros((1, W), F32), jnp.ones((1, W), F32))
        for k in reversed(STEPS):
            same = (ids == row_of(k)).astype(I32) * (1 - taken)
            put_ref[lo : lo + W, k * W : (k + 1) * W] = same.astype(F32).astype(BF)
            taken = taken + jnp.sum(same, axis=1, keepdims=True)
            weight_ref[k : k + 1, lo : lo + W] = scale_row(exps, k, lo, W, tile) * alive
            if k:
                hit = jnp.max((col_of(k) == lane).astype(F32), axis=0, keepdims=True)
                alive = alive * (1.0 - hit)
        base_ref[lo : lo + W, :] = jnp.where(taken > 0, 0.0, cur[lo : lo + W, :].astype(F32)).astype(BF)


def assemble_kernel(scal, piv, own, other, came, rest, top_ref, pick_ref):
    row_of, col_of = pivot_views(piv)
    is_top = scal[ROW] == 0
    low = scal[IS_LOW] == 1
    core0 = scal[CORE] == 0
    half = W // 2
    tops, picks = [], []
    for k in STEPS:
        a = own[k * W : (k + 1) * W, :].astype(F32)
        b = other[k * W : (k + 1) * W, :].astype(F32)
        c = came[k * half : (k + 1) * half, :].astype(F32)
        d = rest[k * half : (k + 1) * half, :].astype(F32)
        got = jnp.concatenate([jnp.where(core0, c, d), jnp.where(core0, d, c)], axis=0)
        tops.append(jnp.where(low, jnp.where(is_top, a, b), got))
        chip = jnp.where(low, jnp.where(is_top, b, a), a + b)
        picks.append(jnp.where(here_column(scal, col_of(k)), chip, got))
    table = matches(STEPS, row_of, col_of)
    chosen = rows_resolved(scal, STEPS, table, col_of, tops, picks)
    for k in STEPS:
        top_ref[k * W : (k + 1) * W, :] = tops[k].astype(BF)
        pick_ref[k * W : (k + 1) * W, :] = chosen[k].astype(BF)


def chain_kernel(n_piece, split, n_side, scal, *refs):
    _, tops, chosen, put, start_rows, inv = refs[:6]
    sides = refs[6 : 6 + n_side]
    refs = refs[6 + n_side :]
    weight, pieces = refs[0], refs[1:n_piece]
    mix_ref, base_ref, s_ref, u_ref = refs[n_piece:]
    row_dev, columns = start_rows.shape
    part = W // n_piece
    top_block = scal[FIRST] == 0
    core0 = scal[CORE] == 0
    def panel_rows(arrays, base):
        if len(arrays) == 1:
            return arrays[0][:, base : base + W]
        line, cross = arrays
        blocks = []
        for z in range(n_piece // 2):
            blocks += [line[z * part : (z + 1) * part, base : base + W], cross[z * part : (z + 1) * part, base : base + W]]
        return jnp.concatenate(blocks, axis=0)

    def side_rows(pair, which):
        base = PAIRS.index(pair) * W
        if not split:
            return panel_rows(sides, base + which * len(PAIRS) * W)
        mine = panel_rows(sides[: n_side // 2], base)
        theirs = panel_rows(sides[n_side // 2 :], base)
        mine_is = core0 if which == 0 else jnp.logical_not(core0)
        return jnp.where(mine_is, mine.astype(F32), theirs.astype(F32)).astype(BF)

    for k in STEPS:
        rows = slice(k * W, (k + 1) * W)
        acc, upper = chosen[rows, :].astype(F32), tops[rows, :].astype(F32)
        for e in STEPS[:k]:
            mixed = mix_ref[e * W : (e + 1) * W, :]
            acc = acc - dot_tn(side_rows((k, e), 1), mixed)
            upper = upper - dot_tn(side_rows((k, e), 0), mixed)
        u_ref[k * W : (k + 1) * W, :] = upper.astype(BF)
        s_ref[k * W : (k + 1) * W, :] = dot(inv[k], acc.astype(BF)).astype(BF)
        for m in range(n_piece):
            if n_piece == 1:
                mix_ref[k * W : (k + 1) * W, :] = s_ref[k * W : (k + 1) * W, :]
                break
            start = pl.multiple_of((scal[ME] ^ m) * part, part)
            mix_ref[k * W + m * part : k * W + (m + 1) * part, :] = s_ref[pl.ds(k * W + start, part), :]

    @pl.when(top_block)
    def _():
        base_ref[...] = s_ref[...].astype(F32)

    @pl.when(jnp.logical_not(top_block))
    def _():
        early = (n_piece - 1) * part
        for lo in range(0, row_dev, W):
            rows = slice(lo, lo + W)
            acc = start_rows[rows, :].astype(F32) + dot(put[rows, :], u_ref[...])
            for k in STEPS:
                if early:
                    block = jnp.concatenate([p[k, :, rows] for p in pieces], axis=0) * weight[k : k + 1, rows].astype(BF)
                    acc = acc - dot_tn(block, mix_ref[k * W : k * W + early, :])
            base_ref[rows, :] = acc


def update_kernel(base, weight, mix, last, out):
    rows = pl.ds(pl.multiple_of(pl.program_id(0) * out.shape[0], out.shape[0]), out.shape[0])
    part = last.shape[1]
    block = jnp.concatenate([last[k, :, rows] * weight[k : k + 1, rows].astype(BF) for k in STEPS], axis=0)
    mixed = jnp.concatenate([mix[(k + 1) * W - part : (k + 1) * W, :] for k in STEPS], axis=0)
    out[...] = (base[...] - dot_tn(block, mixed)).astype(BF)


def place(split, row_dev, n_row, summed):
    row = lax.axis_index("prow")
    me = lax.axis_index("pcol")
    first = row * row_dev
    if split:
        chip = row // 2
        return [first, chip * 2 * row_dev, (chip + 1) * 2 * row_dev, (chip == 0).astype(I32), row, row % 2, me]
    return [first, 0, n_row * row_dev, 1, 1 if summed else row, 0, me]


def call(kernel, where, shapes, n_smem, *args, scratch=()):
    single = not isinstance(shapes, (list, tuple))

    def body(*refs):
        kernel(place(*where), *refs)

    return pl.pallas_call(
        body,
        out_shape=shapes,
        in_specs=[SMEM] * n_smem + [VMEM] * (len(args) - n_smem),
        out_specs=VMEM if single else [VMEM] * len(shapes),
        scratch_shapes=list(scratch),
        cost_estimate=COST,
        compiler_params=pltpu.CompilerParams(vmem_limit_bytes=40 * 1024 * 1024),
    )(*args)


def gather(own, axis):
    return [lax.all_gather(own, "pcol", axis=axis, tiled=True)]


def after(value, *others):
    return lax.optimization_barrier((value,) + others)[0]


def make(n_row, n_col):
    split = n_row == 4 and n_col == 8
    n_piece = 8 if split else 1

    def psum_pair(own, row):
        zero = jnp.zeros_like(own)
        picks = lax.psum(jnp.where(row == 0, zero, own), "prow")
        tops = lax.psum(jnp.where(row == 0, own, zero), "prow")
        return picks.astype(F32).astype(BF), tops.astype(F32).astype(BF)

    def on_device(matrix, panels, exponents, inverses, pivots):
        row_dev, columns = matrix.shape
        assert len(STEPS) * W == row_dev and pivots.shape == (len(STEPS), W)
        tile = row_dev // exponents.shape[1]
        part = W // n_col
        row = lax.axis_index("prow")
        where = (split, row_dev, n_row, False)
        where2 = (split, row_dev, n_row, True)
        wide = len(PAIRS) * W
        bf = lambda *shape: jax.ShapeDtypeStruct(shape, BF)

        sp = call(functools.partial(pass_first, slice_pick_kernel, tile), where, bf(part, wide), 1, exponents, pivots, panels)
        rows = call(row_pick_kernel, where, bf(row_dev, columns), 0, pivots, matrix)
        load = wide if split else 2 * wide
        final_slices = functools.partial(pass_first, slice_final_kernel, split)
        if split:
            sp_other = swap(sp, "prow", 4, 1)
            message = call(slice_message_kernel, where, bf(part, wide), 0, pivots, sp, sp_other)
            sp_came = swap(message, "prow", 4, 2)
        else:
            sp, sp_other = psum_pair(sp, row)
            sp_came = sp
        put, start_rows, weight = call(
            functools.partial(pass_first, prepare_kernel, tile),
            where,
            [bf(row_dev, row_dev), bf(row_dev, columns), jax.ShapeDtypeStruct((8, row_dev), F32)],
            1,
            exponents, after(pivots, sp), matrix,
        )
        if n_piece == 8:
            bz2 = swap(panels, "pcol", 8, 4)
            bx0 = swap(panels, "pcol", 8, 1)
            bz1 = swap(panels, "pcol", 8, 2)
            sp_came = after(sp_came, bx0, weight)
            own = call(final_slices, where2, bf(part, load), 0, pivots, sp, sp_other, sp_came)
        else:
            own = call(final_slices, where2, bf(part, load), 0, pivots, sp, sp_other, sp_came)
            bulk, special = gather(panels, 1), gather(own, 0)
        if split:
            other = swap(rows, "prow", 4, 1)
            message = call(row_message_kernel, where, bf(row_dev // 2, columns), 0, after(pivots, own, bz2), rows, other)
            came = swap(message, "prow", 4, 2)
            rest = None
        else:
            message = rows
            rows, other = psum_pair(rows, row)
            came = rest = rows[: row_dev // 2]
        held = pivots
        if n_piece == 8:
            sz2 = swap(after(own, message, bz1), "pcol", 8, 4)
            sz3 = swap(own, "pcol", 8, 6)
            sz1 = swap(own, "pcol", 8, 2)
            bz3 = swap(after(panels, bz2, sz1), "pcol", 8, 6)
            line = jnp.concatenate([own, sz1, sz2, sz3], axis=0)
            cross = swap(line, "pcol", 8, 1)
            bz2x = swap(after(bz2, sz3), "pcol", 8, 1)
            bz3x = swap(bz3, "pcol", 8, 1)
            line_other = swap(line, "prow", 4, 1)
            bz1x = swap(after(bx0, sz3), "pcol", 8, 2)
            rest = swap(after(came, bz2x, bz1x), "prow", 4, 1)
            bulk = [panels, bx0, bz1, bz1x, bz2, bz2x, bz3, bz3x]
            cross_other = swap(after(cross, bz3), "prow", 4, 1)
            special = [line, cross, line_other, cross_other]
            held = pivots
        elif split:
            special = special + [swap(special[0], "prow", 4, 1)]
        tops, chosen = call(assemble_kernel, where2, [bf(row_dev, columns)] * 2, 0, pivots, rows, other, came, rest)
        mix, base = call(
            functools.partial(chain_kernel, n_piece, split, len(special)),
            where2,
            [bf(row_dev, columns), jax.ShapeDtypeStruct((row_dev, columns), F32)],
            0,
            held, tops, chosen, put, start_rows, inverses, *special, weight, *bulk[:-1],
            scratch=[pltpu.VMEM((row_dev, columns), BF)] * 2,
        )
        return pl.pallas_call(
            update_kernel,
            out_shape=bf(row_dev, columns),
            grid=(row_dev // 512,),
            in_specs=[pl.BlockSpec((512, columns), lambda i: (i, 0))] + [VMEM] * 3,
            out_specs=pl.BlockSpec((512, columns), lambda i: (i, 0)),
            cost_estimate=COST,
            compiler_params=pltpu.CompilerParams(vmem_limit_bytes=40 * 1024 * 1024),
        )(base, weight, mix, bulk[-1])

    return on_device


def solution(mesh):
    return jax.shard_map(
        make(mesh.shape["prow"], mesh.shape["pcol"]),
        mesh=mesh,
        in_specs=(P("prow", "pcol"), P(None, "pcol", "prow"), P(None, "prow"), P(), P()),
        out_specs=P("prow", "pcol"),
        check_vma=False,
    )
```

```python
import functools

import jax
import jax.numpy as jnp
from jax import lax
from jax.experimental import pallas as pl
from jax.experimental.pallas import tpu as pltpu
from jax.sharding import PartitionSpec as P

STEPS = (0, 1, 2, 3)
PAIRS = [(k, e) for k in STEPS for e in STEPS if e < k]
BF = jnp.bfloat16
F32 = jnp.float32
I32 = jnp.int32
W = 256
VMEM = pl.BlockSpec(memory_space=pltpu.VMEM)
SMEM = pl.BlockSpec(memory_space=pltpu.SMEM)
COST = pl.CostEstimate(flops=1000, bytes_accessed=1000, transcendentals=0)
FIRST, LOW, HIGH, IS_LOW, ROW, CORE, ME = range(7)


def swap(value, axis, size, mask):
    return lax.ppermute(value, axis, [(i, i ^ mask) for i in range(size)])


def dot_tn(a, b):
    return lax.dot_general(a, b, (((0,), (0,)), ((), ())), preferred_element_type=F32)


def dot_nt(a, b):
    return lax.dot_general(a, b, (((1,), (1,)), ((), ())), preferred_element_type=F32)


def dot(a, b):
    return jnp.dot(a, b, preferred_element_type=F32)


def pivot_views(piv_ref):
    rows = piv_ref[...]
    both = jnp.concatenate([rows, rows], axis=0)
    columns = jnp.transpose(both)
    return (lambda k: rows[k : k + 1, :]), (lambda k: columns[:, k : k + 1])


def matches(steps, row_of, col_of):
    out = {}
    for k in steps:
        found = jnp.zeros((W, 1), I32)
        terms = []
        for e in reversed([e for e in steps if e < k]):
            same = (col_of(k) == row_of(e)).astype(I32)
            same = same * (1 - found)
            terms.append((e, same.astype(F32).astype(BF)))
            found = found + jnp.sum(same, axis=1, keepdims=True)
        out[k] = (terms, found)
    return out


def later_matches(k, e, steps, row_of, col_of):
    found = jnp.zeros((1, W), I32)
    for q in steps:
        if e < q < k:
            found = jnp.maximum(found, jnp.max((col_of(q) == row_of(k)).astype(I32), axis=0, keepdims=True))
    return found


def scale_row(exp_ref, step, lo, count, tile):
    parts = []
    for t in range(lo // tile, (lo + count) // tile):
        e = exp_ref[step, t]
        scale = jnp.where(e >= 0, jnp.where(e == 1, 2.0, 1.0), jnp.where(e == -1, 0.5, jnp.where(e == -2, 0.25, 0.125)))
        parts.append(jnp.full((1, tile), scale, F32))
    return jnp.concatenate(parts, axis=1) if len(parts) > 1 else parts[0]


def pick_rows(scal, col, source, row_dev):
    lane = lax.broadcasted_iota(I32, (W, row_dev), 1) + scal[FIRST]
    sel = (col == lane).astype(F32).astype(BF)
    return dot(sel, source)


def slice_pick_kernel(tile, scal, fac, piv, pan, sp_ref):
    row_dev = pan.shape[2]
    _, col_of = pivot_views(piv)
    is_top = scal[ROW] == 0
    lane = lax.broadcasted_iota(I32, (W, row_dev), 1) + scal[FIRST]
    for k in STEPS[1:]:
        sel = (col_of(k) == lane).astype(F32).astype(BF)
        scaled = jnp.concatenate([pan[e].astype(F32) * scale_row(fac, e, 0, row_dev, tile) for e in STEPS[:k]], axis=0).astype(BF)
        got = dot_nt(scaled, sel)
        top = scaled[:, k * W : (k + 1) * W].astype(F32)
        value = jnp.where(is_top, top, got).astype(BF)
        part = pan.shape[1]
        for e in STEPS[:k]:
            at = PAIRS.index((k, e))
            sp_ref[:, at * W : (at + 1) * W] = value[e * part : (e + 1) * part]


def row_pick_kernel(scal, piv, mat, v_ref):
    _, col_of = pivot_views(piv)
    is_top = scal[ROW] == 0
    for k in STEPS:
        @pl.when(is_top)
        def _():
            v_ref[k * W : (k + 1) * W, :] = mat[k * W : (k + 1) * W, :]

        @pl.when(jnp.logical_not(is_top))
        def _():
            v_ref[k * W : (k + 1) * W, :] = pick_rows(scal, col_of(k), mat[...], mat.shape[0]).astype(BF)


def pass_first(kernel, first, scal, *refs):
    kernel(first, scal, *refs)


def slices_resolved(scal, piv, tops, picks):
    row_of, col_of = pivot_views(piv)
    out = []
    table = matches(STEPS, row_of, col_of)
    for k, e in PAIRS:
        value = picks[(k, e)]
        between = [(q, m) for q, m in table[k][0] if q > e]
        if between:
            moved = sum(dot_nt(tops[(q, e)].astype(BF), m) for q, m in between)
            p = row_of(k)
            here = (p >= scal[LOW]) & (p < scal[HIGH])
            resolve = (later_matches(k, e, STEPS, row_of, col_of) > 0) & (here | (scal[IS_LOW] == 1))
            value = jnp.where(resolve, moved, value)
        out.append(value)
    return out


def here_lanes(scal, piv, k):
    p = piv[k : k + 1, :]
    return (p >= scal[LOW]) & (p < scal[HIGH])


def slice_message_kernel(scal, piv, own, other, out):
    is_top = scal[ROW] == 0
    low = scal[IS_LOW] == 1
    tops, picks, sums = {}, {}, {}
    for at, pair in enumerate(PAIRS):
        lanes = slice(at * W, (at + 1) * W)
        a, b = own[:, lanes].astype(F32), other[:, lanes].astype(F32)
        tops[pair] = jnp.where(is_top, a, b)
        picks[pair] = jnp.where(is_top, b, a)
        sums[pair] = a + b
    resolved = slices_resolved(scal, piv, tops, picks)
    for at, pair in enumerate(PAIRS):
        from_low = jnp.where(here_lanes(scal, piv, pair[0]), resolved[at], tops[pair])
        out[:, at * W : (at + 1) * W] = jnp.where(low, from_low, sums[pair]).astype(BF)


def slice_final_kernel(split, scal, piv, own, other, came, out):
    is_top = scal[ROW] == 0
    low = scal[IS_LOW] == 1
    tops, picks = {}, {}
    for at, pair in enumerate(PAIRS):
        lanes = slice(at * W, (at + 1) * W)
        a, b, c = own[:, lanes].astype(F32), other[:, lanes].astype(F32), came[:, lanes].astype(F32)
        tops[pair] = jnp.where(low, jnp.where(is_top, a, b), c)
        chip = jnp.where(low, jnp.where(is_top, b, a), a + b)
        picks[pair] = jnp.where(here_lanes(scal, piv, pair[0]), chip, c)
    resolved = slices_resolved(scal, piv, tops, picks)
    width = len(PAIRS) * W
    for at, pair in enumerate(PAIRS):
        if split:
            value = jnp.where(scal[CORE] == 0, tops[pair], resolved[at])
            out[:, at * W : (at + 1) * W] = value.astype(BF)
        else:
            out[:, at * W : (at + 1) * W] = tops[pair].astype(BF)
            out[:, width + at * W : width + (at + 1) * W] = resolved[at].astype(BF)


def rows_resolved(scal, steps, table, col_of, tops, picks):
    out = []
    for at, k in enumerate(steps):
        value = picks[at]
        terms, found = table[k]
        if terms:
            moved = sum(dot(m, tops[steps.index(e)].astype(BF)) for e, m in terms)
            p = col_of(k)
            here = (p >= scal[LOW]) & (p < scal[HIGH])
            value = jnp.where((found > 0) & (here | (scal[IS_LOW] == 1)), moved, value)
        out.append(value)
    return out


def here_column(scal, p):
    return (p >= scal[LOW]) & (p < scal[HIGH])


def row_message_kernel(scal, piv, own, other, out):
    steps = STEPS
    row_of, col_of = pivot_views(piv)
    n = len(steps)
    is_top = scal[ROW] == 0
    low = scal[IS_LOW] == 1
    a = [own[i * W : (i + 1) * W, :].astype(F32) for i in range(n)]
    b = [other[i * W : (i + 1) * W, :].astype(F32) for i in range(n)]
    tops = [jnp.where(is_top, x, y) for x, y in zip(a, b)]
    picks = [jnp.where(is_top, y, x) for x, y in zip(a, b)]
    table = matches(steps, row_of, col_of)
    resolved = rows_resolved(scal, steps, table, col_of, tops, picks)
    half = W // 2
    for i, k in enumerate(steps):
        from_low = jnp.where(here_column(scal, col_of(k)), resolved[i], tops[i])
        value = jnp.where(low, from_low, a[i] + b[i])
        out[i * half : (i + 1) * half, :] = jnp.where(scal[CORE] == 0, value[:half], value[half:]).astype(BF)


def prepare_kernel(tile, scal, exps, piv, cur, put_ref, base_ref, weight_ref):
    row_of, col_of = pivot_views(piv)
    row_dev, columns = cur.shape
    top_block = scal[FIRST] == 0
    for lo in range(0, row_dev, W):
        ids = lax.broadcasted_iota(I32, (W, W), 0) + scal[FIRST] + lo
        lane = lax.broadcasted_iota(I32, (W, W), 1) + scal[FIRST] + lo
        taken = jnp.zeros((W, 1), I32)
        alive = jnp.where(top_block, jnp.zeros((1, W), F32), jnp.ones((1, W), F32))
        for k in reversed(STEPS):
            same = (ids == row_of(k)).astype(I32) * (1 - taken)
            put_ref[lo : lo + W, k * W : (k + 1) * W] = same.astype(F32).astype(BF)
            taken = taken + jnp.sum(same, axis=1, keepdims=True)
            weight_ref[k : k + 1, lo : lo + W] = scale_row(exps, k, lo, W, tile) * alive
            if k:
                hit = jnp.max((col_of(k) == lane).astype(F32), axis=0, keepdims=True)
                alive = alive * (1.0 - hit)
        base_ref[lo : lo + W, :] = jnp.where(taken > 0, 0.0, cur[lo : lo + W, :].astype(F32)).astype(BF)


def assemble_kernel(scal, piv, own, other, came, rest, top_ref, pick_ref):
    row_of, col_of = pivot_views(piv)
    is_top = scal[ROW] == 0
    low = scal[IS_LOW] == 1
    core0 = scal[CORE] == 0
    half = W // 2
    tops, picks = [], []
    for k in STEPS:
        a = own[k * W : (k + 1) * W, :].astype(F32)
        b = other[k * W : (k + 1) * W, :].astype(F32)
        c = came[k * half : (k + 1) * half, :].astype(F32)
        d = rest[k * half : (k + 1) * half, :].astype(F32)
        got = jnp.concatenate([jnp.where(core0, c, d), jnp.where(core0, d, c)], axis=0)
        tops.append(jnp.where(low, jnp.where(is_top, a, b), got))
        chip = jnp.where(low, jnp.where(is_top, b, a), a + b)
        picks.append(jnp.where(here_column(scal, col_of(k)), chip, got))
    table = matches(STEPS, row_of, col_of)
    chosen = rows_resolved(scal, STEPS, table, col_of, tops, picks)
    for k in STEPS:
        top_ref[k * W : (k + 1) * W, :] = tops[k].astype(BF)
        pick_ref[k * W : (k + 1) * W, :] = chosen[k].astype(BF)


def chain_kernel(n_piece, split, n_side, scal, *refs):
    _, tops, chosen, put, start_rows, inv = refs[:6]
    sides = refs[6 : 6 + n_side]
    refs = refs[6 + n_side :]
    weight, pieces = refs[0], refs[1:n_piece]
    mix_ref, base_ref, s_ref, u_ref = refs[n_piece:]
    row_dev, columns = start_rows.shape
    part = W // n_piece
    top_block = scal[FIRST] == 0
    core0 = scal[CORE] == 0
    def panel_rows(arrays, base):
        if len(arrays) == 1:
            return arrays[0][:, base : base + W]
        line, cross = arrays
        blocks = []
        for z in range(n_piece // 2):
            blocks += [line[z * part : (z + 1) * part, base : base + W], cross[z * part : (z + 1) * part, base : base + W]]
        return jnp.concatenate(blocks, axis=0)

    def side_rows(pair, which):
        base = PAIRS.index(pair) * W
        if not split:
            return panel_rows(sides, base + which * len(PAIRS) * W)
        mine = panel_rows(sides[: n_side // 2], base)
        theirs = panel_rows(sides[n_side // 2 :], base)
        mine_is = core0 if which == 0 else jnp.logical_not(core0)
        return jnp.where(mine_is, mine.astype(F32), theirs.astype(F32)).astype(BF)

    for k in STEPS:
        rows = slice(k * W, (k + 1) * W)
        acc, upper = chosen[rows, :].astype(F32), tops[rows, :].astype(F32)
        for e in STEPS[:k]:
            mixed = mix_ref[e * W : (e + 1) * W, :]
            acc = acc - dot_tn(side_rows((k, e), 1), mixed)
            upper = upper - dot_tn(side_rows((k, e), 0), mixed)
        u_ref[k * W : (k + 1) * W, :] = upper.astype(BF)
        s_ref[k * W : (k + 1) * W, :] = dot(inv[k], acc.astype(BF)).astype(BF)
        for m in range(n_piece):
            if n_piece == 1:
                mix_ref[k * W : (k + 1) * W, :] = s_ref[k * W : (k + 1) * W, :]
                break
            start = pl.multiple_of((scal[ME] ^ m) * part, part)
            mix_ref[k * W + m * part : k * W + (m + 1) * part, :] = s_ref[pl.ds(k * W + start, part), :]

    @pl.when(top_block)
    def _():
        base_ref[...] = s_ref[...].astype(F32)

    @pl.when(jnp.logical_not(top_block))
    def _():
        early = (n_piece - 1) * part
        for lo in range(0, row_dev, W):
            rows = slice(lo, lo + W)
            acc = start_rows[rows, :].astype(F32) + dot(put[rows, :], u_ref[...])
            for k in STEPS:
                if early:
                    block = jnp.concatenate([p[k, :, rows] for p in pieces], axis=0) * weight[k : k + 1, rows].astype(BF)
                    acc = acc - dot_tn(block, mix_ref[k * W : k * W + early, :])
            base_ref[rows, :] = acc


def update_kernel(base, weight, mix, last, out):
    rows = pl.ds(pl.multiple_of(pl.program_id(0) * out.shape[0], out.shape[0]), out.shape[0])
    part = last.shape[1]
    block = jnp.concatenate([last[k, :, rows] * weight[k : k + 1, rows].astype(BF) for k in STEPS], axis=0)
    mixed = jnp.concatenate([mix[(k + 1) * W - part : (k + 1) * W, :] for k in STEPS], axis=0)
    out[...] = (base[...] - dot_tn(block, mixed)).astype(BF)


def place(split, row_dev, n_row, summed):
    row = lax.axis_index("prow")
    me = lax.axis_index("pcol")
    first = row * row_dev
    if split:
        chip = row // 2
        return [first, chip * 2 * row_dev, (chip + 1) * 2 * row_dev, (chip == 0).astype(I32), row, row % 2, me]
    return [first, 0, n_row * row_dev, 1, 1 if summed else row, 0, me]


def call(kernel, where, shapes, n_smem, *args, scratch=()):
    single = not isinstance(shapes, (list, tuple))

    def body(*refs):
        kernel(place(*where), *refs)

    return pl.pallas_call(
        body,
        out_shape=shapes,
        in_specs=[SMEM] * n_smem + [VMEM] * (len(args) - n_smem),
        out_specs=VMEM if single else [VMEM] * len(shapes),
        scratch_shapes=list(scratch),
        cost_estimate=COST,
        compiler_params=pltpu.CompilerParams(vmem_limit_bytes=40 * 1024 * 1024),
    )(*args)


def gather(own, axis):
    return [lax.all_gather(own, "pcol", axis=axis, tiled=True)]


def after(value, *others):
    return lax.optimization_barrier((value,) + others)[0]


def make(n_row, n_col):
    split = n_row == 4 and n_col == 8
    n_piece = 8 if split else 1

    def psum_pair(own, row):
        zero = jnp.zeros_like(own)
        picks = lax.psum(jnp.where(row == 0, zero, own), "prow")
        tops = lax.psum(jnp.where(row == 0, own, zero), "prow")
        return picks.astype(F32).astype(BF), tops.astype(F32).astype(BF)

    def on_device(matrix, panels, exponents, inverses, pivots):
        row_dev, columns = matrix.shape
        assert len(STEPS) * W == row_dev and pivots.shape == (len(STEPS), W)
        tile = row_dev // exponents.shape[1]
        part = W // n_col
        row = lax.axis_index("prow")
        where = (split, row_dev, n_row, False)
        where2 = (split, row_dev, n_row, True)
        wide = len(PAIRS) * W
        bf = lambda *shape: jax.ShapeDtypeStruct(shape, BF)

        sp = call(functools.partial(pass_first, slice_pick_kernel, tile), where, bf(part, wide), 1, exponents, pivots, panels)
        rows = call(row_pick_kernel, where, bf(row_dev, columns), 0, pivots, matrix)
        load = wide if split else 2 * wide
        final_slices = functools.partial(pass_first, slice_final_kernel, split)
        if split:
            sp_other = swap(sp, "prow", 4, 1)
            message = call(slice_message_kernel, where, bf(part, wide), 0, pivots, sp, sp_other)
            sp_came = swap(message, "prow", 4, 2)
        else:
            sp, sp_other = psum_pair(sp, row)
            sp_came = sp
        put, start_rows, weight = call(
            functools.partial(pass_first, prepare_kernel, tile),
            where,
            [bf(row_dev, row_dev), bf(row_dev, columns), jax.ShapeDtypeStruct((8, row_dev), F32)],
            1,
            exponents, after(pivots, sp), matrix,
        )
        if n_piece == 8:
            bz2 = swap(panels, "pcol", 8, 4)
            bx0 = swap(panels, "pcol", 8, 1)
            bz1 = swap(panels, "pcol", 8, 2)
            sp_came = after(sp_came, bx0, weight)
            own = call(final_slices, where2, bf(part, load), 0, pivots, sp, sp_other, sp_came)
        else:
            own = call(final_slices, where2, bf(part, load), 0, pivots, sp, sp_other, sp_came)
            bulk, special = gather(panels, 1), gather(own, 0)
        if split:
            other = swap(rows, "prow", 4, 1)
            message = call(row_message_kernel, where, bf(row_dev // 2, columns), 0, after(pivots, own, bz2), rows, other)
            came = swap(message, "prow", 4, 2)
            rest = None
        else:
            message = rows
            rows, other = psum_pair(rows, row)
            came = rest = rows[: row_dev // 2]
        held = pivots
        if n_piece == 8:
            sz2 = swap(after(own, message, bz1), "pcol", 8, 4)
            sz3 = swap(own, "pcol", 8, 6)
            sz1 = swap(own, "pcol", 8, 2)
            bz3 = swap(after(panels, bz2, sz2), "pcol", 8, 6)
            line = jnp.concatenate([own, sz1, sz2, sz3], axis=0)
            cross = swap(line, "pcol", 8, 1)
            bz2x = swap(after(bz2, sz3), "pcol", 8, 1)
            bz3x = swap(bz3, "pcol", 8, 1)
            line_other = swap(line, "prow", 4, 1)
            bz1x = swap(after(bx0, sz1), "pcol", 8, 2)
            rest = swap(after(came, bz2x, bz1x), "prow", 4, 1)
            bulk = [panels, bx0, bz1, bz1x, bz2, bz2x, bz3, bz3x]
            cross_other = swap(after(cross, bz3), "prow", 4, 1)
            special = [line, cross, line_other, cross_other]
            held = pivots
        elif split:
            special = special + [swap(special[0], "prow", 4, 1)]
        tops, chosen = call(assemble_kernel, where2, [bf(row_dev, columns)] * 2, 0, pivots, rows, other, came, rest)
        mix, base = call(
            functools.partial(chain_kernel, n_piece, split, len(special)),
            where2,
            [bf(row_dev, columns), jax.ShapeDtypeStruct((row_dev, columns), F32)],
            0,
            held, tops, chosen, put, start_rows, inverses, *special, weight, *bulk[:-1],
            scratch=[pltpu.VMEM((row_dev, columns), BF)] * 2,
        )
        return pl.pallas_call(
            update_kernel,
            out_shape=bf(row_dev, columns),
            grid=(row_dev // W,),
            in_specs=[pl.BlockSpec((W, columns), lambda i: (i, 0))] + [VMEM] * 3,
            out_specs=pl.BlockSpec((W, columns), lambda i: (i, 0)),
            cost_estimate=COST,
            compiler_params=pltpu.CompilerParams(vmem_limit_bytes=40 * 1024 * 1024),
        )(base, weight, mix, bulk[-1])

    return on_device


def solution(mesh):
    return jax.shard_map(
        make(mesh.shape["prow"], mesh.shape["pcol"]),
        mesh=mesh,
        in_specs=(P("prow", "pcol"), P(None, "pcol", "prow"), P(None, "prow"), P(), P()),
        out_specs=P("prow", "pcol"),
        check_vma=False,
    )
```
